128 devices in a mesh: leaf: 128 (over x, z, y, core).
Axes of the slice: x: 4, y: 4, z: 4, core: 2. Of those that a mesh axis runs over, the one named last changes fastest.
Arguments:
- density: bfloat16 [256, 24, 28, 512], P('leaf'), may hold values from 0.25 to 450
- occupied: int32 [128, 12, 14], P('leaf'), may hold values 0 or 1
- anterpolate: bfloat16 [512, 128], replicated, may hold values from -0.25 to 0.25
- merge_tables: bfloat16 [8, 128, 128], replicated, may hold values from -0.5 to 0.5
- transfer_tables: bfloat16 [158, 128, 128], replicated, may hold values from -0.0390625 to 0.0390625
- near_tables: bfloat16 [14, 512, 512], replicated, may hold values from -0.0546875 to 0.0546875
Outputs:
- potential: bfloat16 [256, 24, 28, 512], P('leaf')
The draws below stay inside these ranges and needn't reach their ends.
All inputs are finite; a program needn't handle non-finite values. No bound on the sum of `occupied` on one device may be relied on, other than what follows from the above.
Results may differ from the reference program's by a relative error of at most 0.014.
Values may be sent and summed in bfloat16 or wider, within the bound.
No kernel may reach another device: no remote copies, remote signals or barrier semaphores. Data moves between devices by JAX's collectives and lax.ppermute only.
A program may use at most 192 MiB of HBM per device.

```python
import math
import jax
import jax.numpy as jnp
import numpy as np
from jax import lax

YL = 24
XL = 28
PTS = 512
K = 128
NZ = 256
ELECTRONS = 172032


def draw_density(key, part):
    key = jax.random.fold_in(key, 7)
    point_key, leaf_key = jax.random.split(key)
    height = (jnp.arange(NZ, dtype=jnp.float32) + 0.5) / NZ
    point_scale = jnp.exp(jax.random.uniform(point_key, (NZ, YL, XL, PTS), jnp.float32, math.log(0.3), math.log(3.0)))
    leaf_scale = jnp.exp(jax.random.uniform(leaf_key, (NZ, YL, XL, 1), jnp.float32, 0.0, math.log(10.0)))
    profile = 1.0 + 2.0 * height
    values = point_scale * leaf_scale * profile[:, None, None, None]
    return values.astype(jnp.bfloat16)


def touch_ends(values, key, low, largest):
    shape = values.shape
    index_at = [jax.random.randint(jax.random.fold_in(key, axis), (), 0, shape[axis]) for axis in range(len(shape))]
    values = values.at[tuple(index_at)].set(low)
    longest = shape.index(max(shape))
    index_at[longest] = (index_at[longest] + 1) % shape[longest]
    return values.at[tuple(index_at)].set(largest)


def noise(stream_key, dims, deviation, bound, kind=jnp.bfloat16):
    values = deviation * jax.random.normal(stream_key, dims, jnp.float32)
    return jnp.clip(values, min=-bound, max=bound).astype(kind)


def setup_inputs(seed: int = 0) -> dict:
    key_of = jax.random.split(jax.random.key(seed), 7)
    return {
        "density": draw_density(jax.random.fold_in(key_of[6], 71), 0),
        "occupied": touch_ends((jax.random.randint(key_of[1], (NZ // 2, YL // 2, XL // 2), 0, 4) < 3).astype(jnp.int32), jax.random.fold_in(key_of[1], 1), 0, 1),
        "anterpolate": noise(key_of[2], (PTS, K), PTS ** -0.5, 0.25),
        "merge_tables": noise(key_of[3], (8, K, K), K ** -0.5, 0.5),
        "transfer_tables": noise(key_of[4], (158, K, K), (189 * K) ** -0.5, 0.0390625),
        "near_tables": noise(key_of[5], (14, PTS, PTS), (27 * PTS) ** -0.5, 0.0546875),
    }


def positive_offsets(radius, minimum):
    listed = []
    for step_z in range(-radius, radius + 1):
        for step_y in range(-radius, radius + 1):
            for step_x in range(-radius, radius + 1):
                offset = (step_z, step_y, step_x)
                if max(abs(step_z), abs(step_y), abs(step_x)) >= minimum and offset > (0, 0, 0):
                    listed.append(offset)
    return listed


def offset_table(radius, minimum, with_centre):
    listed = positive_offsets(radius, minimum)
    base_row = 1 if with_centre else 0
    offset_list = [offset for offset in listed] + [tuple(-component for component in offset) for offset in listed]
    table_rows = [base_row + table_row for table_row in range(len(listed))] * 2
    transposed = [0] * len(listed) + [1] * len(listed)
    if with_centre:
        offset_list = [(0, 0, 0)] + offset_list
        table_rows = [0] + table_rows
        transposed = [0] + transposed
    return np.array(offset_list, np.int32), np.array(table_rows, np.int32), np.array(transposed, np.int32)


def admit_range(shift_by, parity):
    return (shift_by >= -2 - parity) & (shift_by <= 3 - parity)


def offset_sum(padded, tables, radius, extent, offset_list, table_rows, transposed, admit_all):
    extent_z, extent_y, extent_x = extent
    channels = padded.shape[3]
    parity_z = jnp.arange(extent_z, dtype=jnp.int32) % 2
    parity_y = jnp.arange(extent_y, dtype=jnp.int32) % 2
    parity_x = jnp.arange(extent_x, dtype=jnp.int32) % 2
    wide_tables = tables.astype(jnp.float32)

    def advance(running, offset_entry):
        shift_by, table_row, flipped = offset_entry
        start = (shift_by[0] + radius, shift_by[1] + radius, shift_by[2] + radius, jnp.int32(0))
        source_block = lax.dynamic_slice(padded, start, (extent_z, extent_y, extent_x, channels))
        matrix = wide_tables[table_row]
        matrix = jnp.where(flipped > 0, matrix.T, matrix)
        product = jnp.dot(source_block.reshape(-1, channels), matrix, precision=lax.Precision.HIGHEST)
        product = product.reshape(extent_z, extent_y, extent_x, matrix.shape[1])
        if admit_all:
            return running + product, None
        admission = (admit_range(shift_by[0], parity_z)[:, None, None]
                     & admit_range(shift_by[1], parity_y)[None, :, None]
                     & admit_range(shift_by[2], parity_x)[None, None, :])
        return running + jnp.where(admission[..., None], product, 0.0), None

    running = jnp.zeros((extent_z, extent_y, extent_x, tables.shape[2]), jnp.float32)
    running, _ = lax.scan(advance, running, (jnp.asarray(offset_list), jnp.asarray(table_rows), jnp.asarray(transposed)))
    return running


def merge_upward(moments, merge_tables):
    extent_z, extent_y, extent_x, channels = moments.shape
    grouped = moments.reshape(extent_z // 2, 2, extent_y // 2, 2, extent_x // 2, 2, channels)
    grouped = grouped.transpose(0, 2, 4, 1, 3, 5, 6).reshape(-1, 8 * channels)
    merged = jnp.dot(grouped, merge_tables.reshape(8 * channels, channels), preferred_element_type=jnp.float32)
    return merged.astype(jnp.bfloat16).reshape(extent_z // 2, extent_y // 2, extent_x // 2, channels)


def reference(density, occupied, anterpolate, merge_tables, transfer_tables, near_tables):
    parents_present = occupied.astype(jnp.float32)
    presence = jnp.repeat(jnp.repeat(jnp.repeat(parents_present, 2, axis=0), 2, axis=1), 2, axis=2)
    values = density.astype(jnp.float32) * presence[..., None]
    charge = jnp.sum(values)
    scaled = (values * (ELECTRONS * PTS / charge)).astype(jnp.bfloat16)
    moments = jnp.dot(scaled.reshape(-1, PTS), anterpolate, preferred_element_type=jnp.float32)
    moments = moments.astype(jnp.bfloat16).reshape(NZ, YL, XL, K)
    parent_moments = merge_upward(moments, merge_tables)
    offset_list, table_rows, transposed = offset_table(3, 2, False)
    leaf_pad = jnp.pad(moments.astype(jnp.float32), ((3, 3), (3, 3), (3, 3), (0, 0)))
    leaf_local = offset_sum(leaf_pad, transfer_tables, 3, (NZ, YL, XL), offset_list, table_rows, transposed, False)
    parent_pad = jnp.pad(parent_moments.astype(jnp.float32), ((3, 3), (3, 3), (3, 3), (0, 0)))
    parent_local = 0.5 * offset_sum(parent_pad, transfer_tables, 3, (NZ // 2, YL // 2, XL // 2), offset_list, table_rows, transposed, False)
    parent_local = parent_local.astype(jnp.bfloat16)
    children = jnp.einsum("zyxk,cjk->zyxcj", parent_local.astype(jnp.float32), merge_tables.astype(jnp.float32), precision=lax.Precision.HIGHEST)
    children = children.reshape(NZ // 2, YL // 2, XL // 2, 2, 2, 2, K).transpose(0, 3, 1, 4, 2, 5, 6).reshape(NZ, YL, XL, K)
    local_moments = (leaf_local + children).astype(jnp.bfloat16)
    near_list, near_rows, near_flipped = offset_table(1, 1, True)
    near_pad = jnp.pad(scaled.astype(jnp.float32), ((1, 1), (1, 1), (1, 1), (0, 0)))
    near_part = offset_sum(near_pad, near_tables, 1, (NZ, YL, XL), near_list, near_rows, near_flipped, True)
    far_part = jnp.dot(local_moments.reshape(-1, K), anterpolate.T, preferred_element_type=jnp.float32).reshape(NZ, YL, XL, PTS)
    return (presence[..., None] * (near_part + far_part)).astype(jnp.bfloat16)
```

```python
import jax
import jax.numpy as jnp
import numpy as np
from jax import lax
from jax.experimental import pallas as pl
from jax.experimental.pallas import tpu as pltpu
from jax.sharding import PartitionSpec as P

F32 = jnp.float32
BF16 = jnp.bfloat16
GROUP = 16
LINES = 12
ROWS = GROUP * LINES
PTS = 512
K = 128
COARSE = 48
VMEM = pl.BlockSpec(memory_space=pltpu.VMEM)
SMEM = pl.BlockSpec(memory_space=pltpu.SMEM)


def mul(a, b):
    return jnp.dot(a, b, preferred_element_type=F32)


def mul_t(a, b):
    return lax.dot_general(a, b, (((1,), (1,)), ((), ())), preferred_element_type=F32)


def wide(column):
    return jnp.concatenate([column] * 4, axis=1)


def prologue_kernel(density, mask, anterpolate, merge, low, high, parents, partial, stage):
    stage[...] = jnp.zeros_like(stage)
    packs = (low, high)

    def line(yp, total):
        rows = pl.ds(pl.multiple_of(yp * GROUP, GROUP), GROUP)
        present = wide(mask[rows, :])
        for z in range(2):
            for py in range(2):
                for h in range(4):
                    stage[z * 8 + py * 4 + h, 0:28, :] = density[z, 2 * yp + py, :, h * 128 : h * 128 + 128].astype(F32)
        for z in range(2):
            for py in range(2):
                for px in range(2):
                    part = jnp.concatenate(
                        [stage[z * 8 + py * 4 + h, pl.ds(px, GROUP, stride=2), :] for h in range(4)], axis=1
                    )
                    part = part * present
                    total = total + part
                    packs[z][py * 2 + px, rows, 0:PTS] = part.astype(BF16)
        return total

    total = lax.fori_loop(0, LINES, line, jnp.zeros((GROUP, PTS), F32))
    partial[...] = jnp.broadcast_to(jnp.sum(total), partial.shape)
    for z in range(2):
        found = mul(packs[z][:, :, 0:PTS].reshape(4 * ROWS, PTS), anterpolate[...]).astype(BF16)
        found = found.reshape(4, ROWS, K)
        low[:, :, PTS + z * K : PTS + z * K + K] = found
        high[:, :, PTS + z * K : PTS + z * K + K] = found
    parents[...] = merged(low, merge)


def merged(pack, merge):
    children = [pack[c % 4, :, PTS + (c // 4) * K : PTS + (c // 4) * K + K] for c in range(8)]
    return mul(jnp.concatenate(children, axis=1), merge[...]).astype(BF16)


def prologue(density, mask, anterpolate, merge):
    pack = jax.ShapeDtypeStruct((4, ROWS, PTS + 2 * K), BF16)
    return pl.pallas_call(
        prologue_kernel,
        name="prologue",
        out_shape=(
            pack,
            pack,
            jax.ShapeDtypeStruct((ROWS, K), BF16),
            jax.ShapeDtypeStruct((128, 128), F32),
        ),
        in_specs=[VMEM] * 4,
        out_specs=(VMEM,) * 4,
        scratch_shapes=[pltpu.VMEM((16, 32, 128), F32)],
        compiler_params=pltpu.CompilerParams(vmem_limit_bytes=32 << 20),
    )(density, mask, anterpolate, merge)


KEPT = [(3, 0), (3, 1), (3, 2), (3, 3), (1, 3), (2, 3), (1, 1), (1, 2), (2, 1), (2, 2)]
MIRROR = (3, 1, 2, 0)


def taps(before, centre, after):
    ends = before + after
    return [before, 0.5 * (ends + centre), 0.5 * (ends - centre), after]


def outer_weights(tables, outer):
    def chunk(r, _):
        rows = pl.ds(pl.multiple_of(r * 16, 16), 16)
        for h in range(4):
            lanes = slice(h * 128, h * 128 + 128)
            g = [tables[5 + n, rows, lanes].astype(F32) for n in range(9)]
            along_x = [taps(*g[3 * y : 3 * y + 3]) for y in range(3)]
            for c in range(4):
                along_y = taps(along_x[0][c], along_x[1][c], along_x[2][c])
                for b in range(4):
                    outer[b * 4 + c, rows, lanes] = along_y[b].astype(BF16)
        return 0

    lax.fori_loop(0, PTS // 16, chunk, 0)


def inner_weights(tables, outer, inner):
    def block(n, _):
        here = pl.ds(pl.multiple_of((n // 4) * 128, 128), 128)
        there = pl.ds(pl.multiple_of((n % 4) * 128, 128), 128)
        t = [tables[m, here, there].astype(F32) for m in range(5)]
        f = [None] + [tables[m, there, here].astype(F32).T for m in range(1, 5)]
        above = taps(t[2], t[3], t[4])
        below = taps(f[4], f[3], f[2])
        level = taps(f[1], t[0], t[1])
        for k, (b, c) in enumerate(KEPT):
            if b == 3:
                flat = above[c]
            elif b == 1:
                flat = 0.5 * (below[c] + above[c] + level[c])
            else:
                flat = 0.5 * (below[c] + above[c] - level[c])
            ends = outer[b * 4 + c, here, there].astype(F32)
            ends = ends + outer[MIRROR[b] * 4 + MIRROR[c], there, here].astype(F32).T
            inner[k, here, there] = (0.5 * (ends + flat)).astype(BF16)
            inner[10 + k, here, there] = (0.5 * (ends - flat)).astype(BF16)
        return 0

    lax.fori_loop(0, 16, block, 0)


def spread_line(load, store):
    along_y = []
    for px in range(2):
        d0 = load(1, px, -1)
        d1 = load(0, px, 0)
        d2 = load(1, px, 0)
        d3 = load(0, px, 1)
        along_y.append((d0 - d2, d1 + d2, d2 - d1, d1 - d3))
    for b in range(4):
        even = along_y[0][b]
        odd = along_y[1][b]
        store(b * 4 + 0, pltpu.roll(odd, 1, axis=0) - odd)
        store(b * 4 + 1, even + odd)
        store(b * 4 + 2, odd - even)
        store(b * 4 + 3, even - pltpu.roll(even, GROUP - 1, axis=0))


def spread(first, second, combine, spread_ref, base):
    def line(yp, _):
        rows = pl.ds(pl.multiple_of(yp * GROUP, GROUP), GROUP)
        for h in range(4):
            lanes = slice(h * 128, h * 128 + 128)

            def load(py, px, shift):
                near_line = jnp.clip(yp + shift, 0, LINES - 1)
                at = pl.ds(pl.multiple_of(near_line * GROUP, GROUP), GROUP)
                found = combine(
                    first[py * 2 + px, at, lanes].astype(F32), second[py * 2 + px, at, lanes].astype(F32)
                )
                if shift == 0:
                    return found
                inside = (yp + shift >= 0) & (yp + shift < LINES)
                return jnp.where(inside, found, 0.0)

            def store(n, value):
                spread_ref[base + n, rows, lanes] = value.astype(BF16)

            spread_line(load, store)
        return 0

    lax.fori_loop(0, LINES, line, 0)


def gathered_products(product, held, made):
    for b in range(4):
        for c in range(4):
            made[c] = product(b, c)
        p = [made[c] for c in range(4)]
        sides = (p[0] + p[1] + p[2], p[1] - p[2] - p[3])
        for px in range(2):
            value = sides[px]
            if b == 0:
                held[0, px] = value
            elif b == 1:
                held[0, px] += value
                held[1, px] = value
            elif b == 2:
                held[0, px] += value
                held[1, px] -= value
            else:
                held[1, px] -= value


def near_inner_kernel(low, high, tables, near, outer, parts, inner, held, made):
    outer_weights(tables, outer)
    inner_weights(tables, outer, inner)
    spread(low, high, lambda d1, d2: d1 + d2, parts, 0)
    spread(low, high, lambda d1, d2: d2 - d1, parts, 16)

    def product(a):
        def one(b, c):
            left = parts[a * 16 + b * 4 + c]
            if (b, c) in KEPT:
                return mul(left, inner[a * 10 + KEPT.index((b, c))])
            return mul_t(left, inner[a * 10 + KEPT.index((MIRROR[b], MIRROR[c]))])

        return one

    gathered_products(product(0), held, made)
    near[0] = held[...]
    near[1] = held[...]
    gathered_products(product(1), held, made)
    near[0] += held[...]
    near[1] -= held[...]


def near_inner(low, high, tables):
    return pl.pallas_call(
        near_inner_kernel,
        name="near_inner",
        out_shape=(
            jax.ShapeDtypeStruct((2, 2, 2, ROWS, PTS), F32),
            jax.ShapeDtypeStruct((16, PTS, PTS), BF16),
        ),
        in_specs=[VMEM] * 3,
        out_specs=(VMEM,) * 2,
        scratch_shapes=[
            pltpu.VMEM((32, ROWS, PTS), BF16),
            pltpu.VMEM((20, PTS, PTS), BF16),
            pltpu.VMEM((2, 2, ROWS, PTS), F32),
            pltpu.VMEM((4, ROWS, PTS), F32),
        ],
        cost_estimate=pl.CostEstimate(flops=10_000_000_000, bytes_accessed=20_000_000, transcendentals=0),
        compiler_params=pltpu.CompilerParams(vmem_limit_bytes=60 << 20),
    )(low, high, tables)


def near_outer_kernel(kept, low, high, below, above, outer, near_in, near, parts, held, made):
    spread(below, high, lambda d0, d2: d0 * kept[0] - d2, parts, 0)
    spread(low, above, lambda d1, d3: d1 - d3 * kept[1], parts, 16)
    gathered_products(
        lambda b, c: mul_t(parts[b * 4 + c], outer[MIRROR[b] * 4 + MIRROR[c]]), held, made
    )
    near[0] = near_in[0] + held[...]
    gathered_products(lambda b, c: mul(parts[16 + b * 4 + c], outer[b * 4 + c]), held, made)
    near[1] = near_in[1] - held[...]


def near_outer(kept, low, high, below, above, outer, near):
    return pl.pallas_call(
        near_outer_kernel,
        name="near_outer",
        out_shape=jax.ShapeDtypeStruct((2, 2, 2, ROWS, PTS), F32),
        in_specs=[SMEM] + [VMEM] * 6,
        out_specs=VMEM,
        scratch_shapes=[
            pltpu.VMEM((32, ROWS, PTS), BF16),
            pltpu.VMEM((2, 2, ROWS, PTS), F32),
            pltpu.VMEM((4, ROWS, PTS), F32),
        ],
        cost_estimate=pl.CostEstimate(flops=7_000_000_000, bytes_accessed=20_000_000, transcendentals=0),
        compiler_params=pltpu.CompilerParams(vmem_limit_bytes=60 << 20),
    )(kept, low, high, below, above, outer, near)


def positive_offsets(radius, minimum):
    reach = range(-radius, radius + 1)
    return [
        (z, y, x)
        for z in reach
        for y in reach
        for x in reach
        if max(abs(z), abs(y), abs(x)) >= minimum and (z, y, x) > (0, 0, 0)
    ]


RANK = {offset: row for row, offset in enumerate(positive_offsets(3, 2))}


def transfer_terms(tables, dz, reach, py, source):
    plain, flipped = ([], []), ([], [])
    blank = jnp.zeros((K, K), BF16)
    for jy in reach:
        dy = jy - py
        for jx in range(-2, 4):
            pair = []
            for px in range(2):
                offset = (dz, dy, jx - px)
                other = tuple(-d for d in offset)
                pair.append((RANK.get(offset), RANK.get(other)))
            left = None
            for way, kept in ((0, plain), (1, flipped)):
                if pair[0][way] is None and pair[1][way] is None:
                    continue
                left = source(jy, jx) if left is None else left
                kept[0].append(left)
                kept[1].append(
                    jnp.concatenate(
                        [blank if q[way] is None else tables[q[way]] for q in pair], axis=1 - way
                    )
                )
    terms = []
    if plain[0]:
        terms.append(mul(jnp.concatenate(plain[0], axis=1), jnp.concatenate(plain[1], axis=0)))
    if flipped[0]:
        terms.append(mul_t(jnp.concatenate(flipped[0], axis=1), jnp.concatenate(flipped[1], axis=1)))
    return terms


def neighbours(even, odd, count):
    return jnp.concatenate(
        [
            pltpu.roll(even, 1, axis=0),
            pltpu.roll(odd, 1, axis=0),
            even,
            odd,
            pltpu.roll(even, count - 1, axis=0),
            pltpu.roll(odd, count - 1, axis=0),
        ],
        axis=1,
    ).astype(BF16)


def coarse_lines(box, stage, slot, lines):
    stage[...] = box
    sides = []
    for py in range(2):
        halves = []
        for px in range(2):
            halves.append(
                jnp.concatenate(
                    [stage[pl.ds(32 * g + 16 * py + px, 8, stride=2), :] for g in range(6)], axis=0
                )
            )
        sides.append(halves)
    blank = jnp.zeros((8, K), F32)
    for jy in range(-2, 4):
        even, odd = sides[jy % 2]
        if jy // 2 < 0:
            even, odd = [jnp.concatenate([blank, h[: COARSE - 8]], axis=0) for h in (even, odd)]
        elif jy // 2 > 0:
            even, odd = [jnp.concatenate([h[8:], blank], axis=0) for h in (even, odd)]
        lines[slot, jy + 2] = neighbours(even, odd, COARSE)


def transfer_kernel(
    parity, kept, low, below, above, own, back2, ahead2, far3, mask, charge, merge, anterpolate, tables, near,
    potential, leaves, lines, stage, weave, coarse,
):
    packs = (below, below, low, low, above, above)
    leaves[...] = jnp.zeros_like(leaves)
    for n in range(6):
        first = PTS + (n % 2) * K
        for py in range(2):
            even = packs[n][py * 2, :, first : first + K].astype(F32)
            odd = packs[n][py * 2 + 1, :, first : first + K].astype(F32)
            if n < 2 or n > 3:
                even, odd = even * kept[n // 4], odd * kept[n // 4]
            leaves[n, py, GROUP : GROUP + ROWS, :] = neighbours(even, odd, ROWS)
    side = parity[0]
    boxes = (back2[...], merged(below, merge), own[...], merged(above, merge), ahead2[...])
    for n, (box, flag) in enumerate(zip(boxes, (2, 0, None, 1, 3))):
        box = box.astype(F32)
        coarse_lines(box if flag is None else box * kept[flag], stage, n + side, lines)
    coarse_lines(far3[...].astype(F32) * kept[4], stage, 5 - 5 * side, lines)

    for pz in range(2):

        @pl.when(side == pz)
        def _():
            for py in range(2):
                total = None
                for jz in range(-2, 4):
                    for term in transfer_terms(
                        tables,
                        jz - pz,
                        range(-2, 4),
                        py,
                        lambda jy, jx: lines[jz + 2, jy + 2, :, (jx + 2) * K : (jx + 3) * K],
                    ):
                        total = term if total is None else total + term
                coarse[py] = 0.5 * total

    for py in range(2):
        for px in range(2):
            for g in range(6):
                stage[pl.ds(32 * g + 16 * py + px, 8, stride=2), :] = coarse[
                    py, g * 8 : g * 8 + 8, px * K : px * K + K
                ]
    parent_local = stage[...].astype(BF16)

    total_charge = jnp.sum(charge[...], axis=0, keepdims=True)
    leaf_count = 2.0 * 24 * 28 * 128
    factor = wide(mask[...] * (leaf_count * PTS / total_charge))

    for pz in range(2):
        for py in range(2):
            total = mul_t(parent_local, merge[(4 * pz + 2 * py) * K : (4 * pz + 2 * py) * K + 2 * K, :])
            for jz in range(-2, 4):
                for term in transfer_terms(
                    tables,
                    jz - pz,
                    range(-2, 4),
                    py,
                    lambda jy, jx: leaves[
                        jz + 2,
                        jy % 2,
                        GROUP * (1 + jy // 2) : GROUP * (1 + jy // 2) + ROWS,
                        (jx + 2) * K : (jx + 3) * K,
                    ],
                ):
                    total = total + term
            local = total.astype(BF16)
            for px in range(2):
                far = mul_t(local[:, px * K : px * K + K], anterpolate[...])
                found = (near[pz, py, px] + far) * factor
                for yp in range(LINES):
                    for h in range(4):
                        weave[yp * 4 + h, pl.ds(px, GROUP, stride=2), :] = found[
                            yp * GROUP : yp * GROUP + GROUP, h * 128 : h * 128 + 128
                        ]
            for yp in range(LINES):
                for h in range(4):
                    potential[pz, 2 * yp + py, :, h * 128 : h * 128 + 128] = weave[yp * 4 + h, 0:28, :].astype(BF16)


def transfer(parity, kept, low, below, above, own, back2, ahead2, far3, mask, charge, merge, anterpolate, tables, near):
    return pl.pallas_call(
        transfer_kernel,
        name="transfer",
        out_shape=jax.ShapeDtypeStruct((2, 2 * LINES, 28, PTS), BF16),
        in_specs=[SMEM] * 2 + [VMEM] * 13,
        out_specs=VMEM,
        scratch_shapes=[
            pltpu.VMEM((6, 2, ROWS + 2 * GROUP, 6 * K), BF16),
            pltpu.VMEM((6, 6, COARSE, 6 * K), BF16),
            pltpu.VMEM((ROWS, K), F32),
            pltpu.VMEM((LINES * 4, 32, 128), F32),
            pltpu.VMEM((2, COARSE, 2 * K), F32),
        ],
        cost_estimate=pl.CostEstimate(flops=12_000_000_000, bytes_accessed=20_000_000, transcendentals=0),
        compiler_params=pltpu.CompilerParams(vmem_limit_bytes=60 << 20),
    )(parity, kept, low, below, above, own, back2, ahead2, far3, mask, charge, merge, anterpolate, tables, near)


def around(count, step):
    return [(i, (i + step) % count) for i in range(count)]


def body(density, occupied, anterpolate, merge_tables, transfer_tables, near_tables):
    count = lax.axis_size("leaf")
    present = jnp.pad(occupied[0].astype(F32), ((0, 0), (0, GROUP - occupied.shape[2])))
    mask = jnp.broadcast_to(present.reshape(ROWS, 1), (ROWS, 128))
    merge = merge_tables.reshape(8 * K, K)
    low, high, own, partial = prologue(density, mask, anterpolate, merge)
    place = lax.axis_index("leaf")
    below = lax.ppermute(high, "leaf", around(count, 1))
    above = lax.ppermute(low, "leaf", around(count, -1))
    back2 = lax.ppermute(own, "leaf", around(count, 2))
    ahead2 = lax.ppermute(own, "leaf", around(count, -2))
    crossed = [(i, (i + 3) % count) for i in range(0, count, 2)]
    far3 = lax.ppermute(own, "leaf", crossed + [(j, i) for i, j in crossed])
    charge = lax.all_to_all(partial, "leaf", 0, 0, tiled=True)
    parity = place % 2
    source3 = place + 3 - 6 * parity
    kept = jnp.stack(
        [place >= 1, place < count - 1, place >= 2, place < count - 2, (source3 >= 0) & (source3 < count)]
    ).astype(F32)
    near, outer = near_inner(low, high, near_tables)
    near = near_outer(kept, low, high, below, above, outer, near)
    return transfer(
        parity.reshape(1), kept, low, below, above, own, back2, ahead2, far3, mask, charge, merge, anterpolate,
        transfer_tables, near,
    )


def solution(mesh):
    return jax.shard_map(
        body,
        mesh=mesh,
        in_specs=(P("leaf", None, None, None), P("leaf", None, None), P(), P(), P(), P()),
        out_specs=P("leaf", None, None, None),
        check_vma=False,
    )
```

```python
import jax
import jax.numpy as jnp
import numpy as np
from jax import lax
from jax.experimental import pallas as pl
from jax.experimental.pallas import tpu as pltpu
from jax.sharding import PartitionSpec as P

F32 = jnp.float32
BF16 = jnp.bfloat16
GROUP = 16
LINES = 12
ROWS = GROUP * LINES
PTS = 512
K = 128
COARSE = 48
VMEM = pl.BlockSpec(memory_space=pltpu.VMEM)
SMEM = pl.BlockSpec(memory_space=pltpu.SMEM)
ANY = pl.BlockSpec(memory_space=pl.ANY)


def mul(a, b):
    return jnp.dot(a, b, preferred_element_type=F32)


def mul_t(a, b):
    return lax.dot_general(a, b, (((1,), (1,)), ((), ())), preferred_element_type=F32)


def wide(column):
    return jnp.concatenate([column] * 4, axis=1)


def prologue_kernel(density, mask, anterpolate, merge, low, high, parents, partial, stage):
    stage[...] = jnp.zeros_like(stage)
    packs = (low, high)

    def line(yp, total):
        rows = pl.ds(pl.multiple_of(yp * GROUP, GROUP), GROUP)
        present = wide(mask[rows, :])
        for z in range(2):
            for py in range(2):
                for h in range(4):
                    stage[z * 8 + py * 4 + h, 0:28, :] = density[z, 2 * yp + py, :, h * 128 : h * 128 + 128].astype(F32)
        for z in range(2):
            for py in range(2):
                for px in range(2):
                    part = jnp.concatenate(
                        [stage[z * 8 + py * 4 + h, pl.ds(px, GROUP, stride=2), :] for h in range(4)], axis=1
                    )
                    part = part * present
                    total = total + part
                    packs[z][py * 2 + px, rows, 0:PTS] = part.astype(BF16)
        return total

    total = lax.fori_loop(0, LINES, line, jnp.zeros((GROUP, PTS), F32))
    partial[...] = jnp.broadcast_to(jnp.sum(total), partial.shape)
    for z in range(2):
        found = mul(packs[z][:, :, 0:PTS].reshape(4 * ROWS, PTS), anterpolate[...]).astype(BF16)
        found = found.reshape(4, ROWS, K)
        low[:, :, PTS + z * K : PTS + z * K + K] = found
        high[:, :, PTS + z * K : PTS + z * K + K] = found
    parents[...] = merged(low, merge)


def merged(pack, merge):
    children = [pack[c % 4, :, PTS + (c // 4) * K : PTS + (c // 4) * K + K] for c in range(8)]
    return mul(jnp.concatenate(children, axis=1), merge[...]).astype(BF16)


def prologue(density, mask, anterpolate, merge):
    pack = jax.ShapeDtypeStruct((4, ROWS, PTS + 2 * K), BF16)
    return pl.pallas_call(
        prologue_kernel,
        name="prologue",
        out_shape=(
            pack,
            pack,
            jax.ShapeDtypeStruct((ROWS, K), BF16),
            jax.ShapeDtypeStruct((128, 128), F32),
        ),
        in_specs=[VMEM] * 4,
        out_specs=(VMEM,) * 4,
        scratch_shapes=[pltpu.VMEM((16, 32, 128), F32)],
        compiler_params=pltpu.CompilerParams(vmem_limit_bytes=32 << 20),
    )(density, mask, anterpolate, merge)


KEPT = [(3, 0), (3, 1), (3, 2), (3, 3), (1, 3), (2, 3), (1, 1), (1, 2), (2, 1), (2, 2)]
MIRROR = (3, 1, 2, 0)


def taps(before, centre, after):
    ends = before + after
    return [before, 0.5 * (ends + centre), 0.5 * (ends - centre), after]


def outer_weights(tables, outer):
    def chunk(r, _):
        rows = pl.ds(pl.multiple_of(r * 16, 16), 16)
        for h in range(4):
            lanes = slice(h * 128, h * 128 + 128)
            g = [tables[5 + n, rows, lanes].astype(F32) for n in range(9)]
            along_x = [taps(*g[3 * y : 3 * y + 3]) for y in range(3)]
            for c in range(4):
                along_y = taps(along_x[0][c], along_x[1][c], along_x[2][c])
                for b in range(4):
                    outer[b * 4 + c, rows, lanes] = along_y[b].astype(BF16)
        return 0

    lax.fori_loop(0, PTS // 16, chunk, 0)


def inner_weights(tables, outer, inner):
    def block(n, _):
        here = pl.ds(pl.multiple_of((n // 4) * 128, 128), 128)
        there = pl.ds(pl.multiple_of((n % 4) * 128, 128), 128)
        t = [tables[m, here, there].astype(F32) for m in range(5)]
        f = [None] + [tables[m, there, here].astype(F32).T for m in range(1, 5)]
        above = taps(t[2], t[3], t[4])
        below = taps(f[4], f[3], f[2])
        level = taps(f[1], t[0], t[1])
        for k, (b, c) in enumerate(KEPT):
            if b == 3:
                flat = above[c]
            elif b == 1:
                flat = 0.5 * (below[c] + above[c] + level[c])
            else:
                flat = 0.5 * (below[c] + above[c] - level[c])
            ends = outer[b * 4 + c, here, there].astype(F32)
            ends = ends + outer[MIRROR[b] * 4 + MIRROR[c], there, here].astype(F32).T
            inner[k, here, there] = (0.5 * (ends + flat)).astype(BF16)
            inner[10 + k, here, there] = (0.5 * (ends - flat)).astype(BF16)
        return 0

    lax.fori_loop(0, 16, block, 0)


def spread_line(load, store):
    along_y = []
    for px in range(2):
        d0 = load(1, px, -1)
        d1 = load(0, px, 0)
        d2 = load(1, px, 0)
        d3 = load(0, px, 1)
        along_y.append((d0 - d2, d1 + d2, d2 - d1, d1 - d3))
    for b in range(4):
        even = along_y[0][b]
        odd = along_y[1][b]
        store(b * 4 + 0, pltpu.roll(odd, 1, axis=0) - odd)
        store(b * 4 + 1, even + odd)
        store(b * 4 + 2, odd - even)
        store(b * 4 + 3, even - pltpu.roll(even, GROUP - 1, axis=0))


def spread(first, second, combine, spread_ref, base):
    def line(yp, _):
        rows = pl.ds(pl.multiple_of(yp * GROUP, GROUP), GROUP)
        for h in range(4):
            lanes = slice(h * 128, h * 128 + 128)

            def load(py, px, shift):
                near_line = jnp.clip(yp + shift, 0, LINES - 1)
                at = pl.ds(pl.multiple_of(near_line * GROUP, GROUP), GROUP)
                found = combine(
                    first[py * 2 + px, at, lanes].astype(F32), second[py * 2 + px, at, lanes].astype(F32)
                )
                if shift == 0:
                    return found
                inside = (yp + shift >= 0) & (yp + shift < LINES)
                return jnp.where(inside, found, 0.0)

            def store(n, value):
                spread_ref[base + n, rows, lanes] = value.astype(BF16)

            spread_line(load, store)
        return 0

    lax.fori_loop(0, LINES, line, 0)


def gathered_products(product, held, made):
    for b in range(4):
        for c in range(4):
            made[c] = product(b, c)
        p = [made[c] for c in range(4)]
        sides = (p[0] + p[1] + p[2], p[1] - p[2] - p[3])
        for px in range(2):
            value = sides[px]
            if b == 0:
                held[0, px] = value
            elif b == 1:
                held[0, px] += value
                held[1, px] = value
            elif b == 2:
                held[0, px] += value
                held[1, px] -= value
            else:
                held[1, px] -= value


def near_inner_kernel(low, high, tables_in, near, outer_out, parts, inner, held, made, tables, outer, sems):
    ends = pltpu.make_async_copy(tables_in.at[5:14], tables.at[5:14], sems.at[0])
    flats = pltpu.make_async_copy(tables_in.at[0:5], tables.at[0:5], sems.at[1])
    ends.start()
    flats.start()
    spread(low, high, lambda d1, d2: d1 + d2, parts, 0)
    spread(low, high, lambda d1, d2: d2 - d1, parts, 16)
    ends.wait()
    outer_weights(tables, outer)
    leaving = pltpu.make_async_copy(outer, outer_out, sems.at[2])
    leaving.start()
    flats.wait()
    inner_weights(tables, outer, inner)

    def product(a):
        def one(b, c):
            left = parts[a * 16 + b * 4 + c]
            if (b, c) in KEPT:
                return mul(left, inner[a * 10 + KEPT.index((b, c))])
            return mul_t(left, inner[a * 10 + KEPT.index((MIRROR[b], MIRROR[c]))])

        return one

    gathered_products(product(0), held, made)
    near[0] = held[...]
    near[1] = held[...]
    gathered_products(product(1), held, made)
    near[0] += held[...]
    near[1] -= held[...]
    leaving.wait()


def near_inner(low, high, tables):
    return pl.pallas_call(
        near_inner_kernel,
        name="near_inner",
        out_shape=(
            jax.ShapeDtypeStruct((2, 2, 2, ROWS, PTS), F32),
            jax.ShapeDtypeStruct((16, PTS, PTS), BF16),
        ),
        in_specs=[VMEM, VMEM, ANY],
        out_specs=(VMEM, ANY),
        scratch_shapes=[
            pltpu.VMEM((32, ROWS, PTS), BF16),
            pltpu.VMEM((20, PTS, PTS), BF16),
            pltpu.VMEM((2, 2, ROWS, PTS), F32),
            pltpu.VMEM((4, ROWS, PTS), F32),
            pltpu.VMEM((14, PTS, PTS), BF16),
            pltpu.VMEM((16, PTS, PTS), BF16),
            pltpu.SemaphoreType.DMA((3,)),
        ],
        cost_estimate=pl.CostEstimate(flops=10_000_000_000, bytes_accessed=20_000_000, transcendentals=0),
        compiler_params=pltpu.CompilerParams(vmem_limit_bytes=60 << 20),
    )(low, high, tables)


def near_outer_kernel(kept, low, high, below, above, outer_in, near_in, near, parts, held, made, outer, sems):
    weights = pltpu.make_async_copy(outer_in, outer, sems.at[0])
    inner_part = pltpu.make_async_copy(near_in, near, sems.at[1])
    weights.start()
    inner_part.start()
    spread(below, high, lambda d0, d2: d0 * kept[0] - d2, parts, 0)
    spread(low, above, lambda d1, d3: d1 - d3 * kept[1], parts, 16)
    weights.wait()
    gathered_products(
        lambda b, c: mul_t(parts[b * 4 + c], outer[MIRROR[b] * 4 + MIRROR[c]]), held, made
    )
    inner_part.wait()
    near[0] += held[...]
    gathered_products(lambda b, c: mul(parts[16 + b * 4 + c], outer[b * 4 + c]), held, made)
    near[1] -= held[...]


def near_outer(kept, low, high, below, above, outer, near):
    return pl.pallas_call(
        near_outer_kernel,
        name="near_outer",
        out_shape=jax.ShapeDtypeStruct((2, 2, 2, ROWS, PTS), F32),
        in_specs=[SMEM] + [VMEM] * 4 + [ANY] * 2,
        out_specs=VMEM,
        scratch_shapes=[
            pltpu.VMEM((32, ROWS, PTS), BF16),
            pltpu.VMEM((2, 2, ROWS, PTS), F32),
            pltpu.VMEM((4, ROWS, PTS), F32),
            pltpu.VMEM((16, PTS, PTS), BF16),
            pltpu.SemaphoreType.DMA((2,)),
        ],
        cost_estimate=pl.CostEstimate(flops=7_000_000_000, bytes_accessed=20_000_000, transcendentals=0),
        compiler_params=pltpu.CompilerParams(vmem_limit_bytes=60 << 20),
    )(kept, low, high, below, above, outer, near)


def positive_offsets(radius, minimum):
    reach = range(-radius, radius + 1)
    return [
        (z, y, x)
        for z in reach
        for y in reach
        for x in reach
        if max(abs(z), abs(y), abs(x)) >= minimum and (z, y, x) > (0, 0, 0)
    ]


RANK = {offset: row for row, offset in enumerate(positive_offsets(3, 2))}


def transfer_terms(tables, dz, reach, py, source):
    plain, flipped = ([], []), ([], [])
    blank = jnp.zeros((K, K), BF16)
    for jy in reach:
        dy = jy - py
        for jx in range(-2, 4):
            pair = []
            for px in range(2):
                offset = (dz, dy, jx - px)
                other = tuple(-d for d in offset)
                pair.append((RANK.get(offset), RANK.get(other)))
            left = None
            for way, kept in ((0, plain), (1, flipped)):
                if pair[0][way] is None and pair[1][way] is None:
                    continue
                left = source(jy, jx) if left is None else left
                kept[0].append(left)
                kept[1].append(
                    jnp.concatenate(
                        [blank if q[way] is None else tables[q[way]] for q in pair], axis=1 - way
                    )
                )
    terms = []
    if plain[0]:
        terms.append(mul(jnp.concatenate(plain[0], axis=1), jnp.concatenate(plain[1], axis=0)))
    if flipped[0]:
        terms.append(mul_t(jnp.concatenate(flipped[0], axis=1), jnp.concatenate(flipped[1], axis=1)))
    return terms


def neighbours(even, odd, count):
    return jnp.concatenate(
        [
            pltpu.roll(even, 1, axis=0),
            pltpu.roll(odd, 1, axis=0),
            even,
            odd,
            pltpu.roll(even, count - 1, axis=0),
            pltpu.roll(odd, count - 1, axis=0),
        ],
        axis=1,
    ).astype(BF16)


def coarse_lines(box, stage, slot, lines):
    stage[...] = box
    sides = []
    for py in range(2):
        halves = []
        for px in range(2):
            halves.append(
                jnp.concatenate(
                    [stage[pl.ds(32 * g + 16 * py + px, 8, stride=2), :] for g in range(6)], axis=0
                )
            )
        sides.append(halves)
    blank = jnp.zeros((8, K), F32)
    for jy in range(-2, 4):
        even, odd = sides[jy % 2]
        if jy // 2 < 0:
            even, odd = [jnp.concatenate([blank, h[: COARSE - 8]], axis=0) for h in (even, odd)]
        elif jy // 2 > 0:
            even, odd = [jnp.concatenate([h[8:], blank], axis=0) for h in (even, odd)]
        lines[slot, jy + 2] = neighbours(even, odd, COARSE)


def transfer_kernel(
    parity, kept, low, below, above, own, back2, ahead2, far3, mask, charge, merge, anterpolate, tables_in, near_in,
    potential, leaves, lines, stage, weave, coarse, tables, near, fine, sems,
):
    operators = pltpu.make_async_copy(tables_in, tables, sems.at[0])
    near_part = pltpu.make_async_copy(near_in, near, sems.at[1])
    operators.start()
    near_part.start()
    packs = (below, below, low, low, above, above)
    leaves[...] = jnp.zeros_like(leaves)
    for n in range(6):
        first = PTS + (n % 2) * K
        for py in range(2):
            even = packs[n][py * 2, :, first : first + K].astype(F32)
            odd = packs[n][py * 2 + 1, :, first : first + K].astype(F32)
            if n < 2 or n > 3:
                even, odd = even * kept[n // 4], odd * kept[n // 4]
            leaves[n, py, GROUP : GROUP + ROWS, :] = neighbours(even, odd, ROWS)
    side = parity[0]
    boxes = (back2[...], merged(below, merge), own[...], merged(above, merge), ahead2[...])
    for n, (box, flag) in enumerate(zip(boxes, (2, 0, None, 1, 3))):
        box = box.astype(F32)
        coarse_lines(box if flag is None else box * kept[flag], stage, n + side, lines)
    coarse_lines(far3[...].astype(F32) * kept[4], stage, 5 - 5 * side, lines)

    operators.wait()
    for pz in range(2):

        @pl.when(side == pz)
        def _():
            for py in range(2):
                total = None
                for jz in range(-2, 4):
                    for term in transfer_terms(
                        tables,
                        jz - pz,
                        range(-2, 4),
                        py,
                        lambda jy, jx: lines[jz + 2, jy + 2, :, (jx + 2) * K : (jx + 3) * K],
                    ):
                        total = term if total is None else total + term
                coarse[py] = 0.5 * total

    for py in range(2):
        for px in range(2):
            for g in range(6):
                stage[pl.ds(32 * g + 16 * py + px, 8, stride=2), :] = coarse[
                    py, g * 8 : g * 8 + 8, px * K : px * K + K
                ]
    parent_local = stage[...].astype(BF16)

    total_charge = jnp.sum(charge[...], axis=0, keepdims=True)
    leaf_count = 2.0 * 24 * 28 * 128
    factor = wide(mask[...] * (leaf_count * PTS / total_charge))

    for py in range(2):
        for pz in range(2):
            first = (4 * pz + 2 * py) * K
            fine[pz * 2 + py] = mul_t(parent_local, merge[first : first + 2 * K, :])
        for dz in range(-3, 4):
            layers = [pz for pz in range(2) if -2 <= dz + pz <= 3]

            def source(jy, jx):
                lines_here = pl.ds(GROUP * (1 + jy // 2), ROWS)
                here = [leaves[dz + pz + 2, jy % 2, lines_here, (jx + 2) * K : (jx + 3) * K] for pz in layers]
                return jnp.concatenate(here, axis=0)

            for term in transfer_terms(tables, dz, range(-2, 4), py, source):
                for n, pz in enumerate(layers):
                    fine[pz * 2 + py] += term[n * ROWS : n * ROWS + ROWS]

    near_part.wait()
    for pz in range(2):
        for py in range(2):
            total = fine[pz * 2 + py]
            local = total.astype(BF16)
            for px in range(2):
                far = mul_t(local[:, px * K : px * K + K], anterpolate[...])
                found = (near[pz, py, px] + far) * factor
                for yp in range(LINES):
                    for h in range(4):
                        weave[yp * 4 + h, pl.ds(px, GROUP, stride=2), :] = found[
                            yp * GROUP : yp * GROUP + GROUP, h * 128 : h * 128 + 128
                        ]
            for yp in range(LINES):
                for h in range(4):
                    potential[pz, 2 * yp + py, :, h * 128 : h * 128 + 128] = weave[yp * 4 + h, 0:28, :].astype(BF16)


def transfer(parity, kept, low, below, above, own, back2, ahead2, far3, mask, charge, merge, anterpolate, tables, near):
    return pl.pallas_call(
        transfer_kernel,
        name="transfer",
        out_shape=jax.ShapeDtypeStruct((2, 2 * LINES, 28, PTS), BF16),
        in_specs=[SMEM] * 2 + [VMEM] * 11 + [ANY] * 2,
        out_specs=VMEM,
        scratch_shapes=[
            pltpu.VMEM((6, 2, ROWS + 2 * GROUP, 6 * K), BF16),
            pltpu.VMEM((6, 6, COARSE, 6 * K), BF16),
            pltpu.VMEM((ROWS, K), F32),
            pltpu.VMEM((LINES * 4, 32, 128), F32),
            pltpu.VMEM((2, COARSE, 2 * K), F32),
            pltpu.VMEM((len(RANK), K, K), BF16),
            pltpu.VMEM((2, 2, 2, ROWS, PTS), F32),
            pltpu.VMEM((4, ROWS, 2 * K), F32),
            pltpu.SemaphoreType.DMA((2,)),
        ],
        cost_estimate=pl.CostEstimate(flops=12_000_000_000, bytes_accessed=20_000_000, transcendentals=0),
        compiler_params=pltpu.CompilerParams(vmem_limit_bytes=60 << 20),
    )(parity, kept, low, below, above, own, back2, ahead2, far3, mask, charge, merge, anterpolate, tables, near)


def around(count, step):
    return [(i, (i + step) % count) for i in range(count)]


def body(density, occupied, anterpolate, merge_tables, transfer_tables, near_tables):
    count = lax.axis_size("leaf")
    present = jnp.pad(occupied[0].astype(F32), ((0, 0), (0, GROUP - occupied.shape[2])))
    mask = jnp.broadcast_to(present.reshape(ROWS, 1), (ROWS, 128))
    merge = merge_tables.reshape(8 * K, K)
    low, high, own, partial = prologue(density, mask, anterpolate, merge)
    place = lax.axis_index("leaf")
    below = lax.ppermute(high, "leaf", around(count, 1))
    above = lax.ppermute(low, "leaf", around(count, -1))
    back2 = lax.ppermute(own, "leaf", around(count, 2))
    ahead2 = lax.ppermute(own, "leaf", around(count, -2))
    crossed = [(i, (i + 3) % count) for i in range(0, count, 2)]
    far3 = lax.ppermute(own, "leaf", crossed + [(j, i) for i, j in crossed])
    parity = place % 2
    source3 = place + 3 - 6 * parity
    kept = jnp.stack(
        [place >= 1, place < count - 1, place >= 2, place < count - 2, (source3 >= 0) & (source3 < count)]
    ).astype(F32)
    near, outer = near_inner(low, high, near_tables)
    partial, near = lax.optimization_barrier((partial, near))
    charge = lax.all_to_all(partial, "leaf", 0, 0, tiled=True)
    near = near_outer(kept, low, high, below, above, outer, near)
    return transfer(
        parity.reshape(1), kept, low, below, above, own, back2, ahead2, far3, mask, charge, merge, anterpolate,
        transfer_tables, near,
    )


def solution(mesh):
    return jax.shard_map(
        body,
        mesh=mesh,
        in_specs=(P("leaf", None, None, None), P("leaf", None, None), P(), P(), P(), P()),
        out_specs=P("leaf", None, None, None),
        check_vma=False,
    )
```

```python
import jax
import jax.numpy as jnp
import numpy as np
from jax import lax
from jax.experimental import pallas as pl
from jax.experimental.pallas import tpu as pltpu
from jax.sharding import PartitionSpec as P

F32 = jnp.float32
BF16 = jnp.bfloat16
GROUP = 16
LINES = 12
ROWS = GROUP * LINES
PTS = 512
K = 128
COARSE = 48
VMEM = pl.BlockSpec(memory_space=pltpu.VMEM)
SMEM = pl.BlockSpec(memory_space=pltpu.SMEM)
ANY = pl.BlockSpec(memory_space=pl.ANY)


def mul(a, b):
    return jnp.dot(a, b, preferred_element_type=F32)


def mul_t(a, b):
    return lax.dot_general(a, b, (((1,), (1,)), ((), ())), preferred_element_type=F32)


def wide(column):
    return jnp.concatenate([column] * 4, axis=1)


def prologue_kernel(density, mask, anterpolate, merge, low, high, parents, partial, stage):
    stage[...] = jnp.zeros_like(stage)
    packs = (low, high)

    def line(yp, total):
        rows = pl.ds(pl.multiple_of(yp * GROUP, GROUP), GROUP)
        present = wide(mask[rows, :])
        for z in range(2):
            for py in range(2):
                for h in range(4):
                    stage[z * 8 + py * 4 + h, 0:28, :] = density[z, 2 * yp + py, :, h * 128 : h * 128 + 128].astype(F32)
        for z in range(2):
            for py in range(2):
                for px in range(2):
                    part = jnp.concatenate(
                        [stage[z * 8 + py * 4 + h, pl.ds(px, GROUP, stride=2), :] for h in range(4)], axis=1
                    )
                    part = part * present
                    total = total + part
                    packs[z][py * 2 + px, rows, 0:PTS] = part.astype(BF16)
        return total

    total = lax.fori_loop(0, LINES, line, jnp.zeros((GROUP, PTS), F32))
    partial[...] = jnp.broadcast_to(jnp.sum(total), partial.shape)
    for z in range(2):
        found = mul(packs[z][:, :, 0:PTS].reshape(4 * ROWS, PTS), anterpolate[...]).astype(BF16)
        found = found.reshape(4, ROWS, K)
        low[:, :, PTS + z * K : PTS + z * K + K] = found
        high[:, :, PTS + z * K : PTS + z * K + K] = found
    parents[...] = merged(low, merge)


def merged(pack, merge):
    children = [pack[c % 4, :, PTS + (c // 4) * K : PTS + (c // 4) * K + K] for c in range(8)]
    return mul(jnp.concatenate(children, axis=1), merge[...]).astype(BF16)


def prologue(density, mask, anterpolate, merge):
    pack = jax.ShapeDtypeStruct((4, ROWS, PTS + 2 * K), BF16)
    return pl.pallas_call(
        prologue_kernel,
        name="prologue",
        out_shape=(
            pack,
            pack,
            jax.ShapeDtypeStruct((ROWS, K), BF16),
            jax.ShapeDtypeStruct((128, 128), F32),
        ),
        in_specs=[VMEM] * 4,
        out_specs=(VMEM,) * 4,
        scratch_shapes=[pltpu.VMEM((16, 32, 128), F32)],
        compiler_params=pltpu.CompilerParams(vmem_limit_bytes=32 << 20),
    )(density, mask, anterpolate, merge)


KEPT = [(3, 0), (3, 1), (3, 2), (3, 3), (1, 3), (2, 3), (1, 1), (1, 2), (2, 1), (2, 2)]
MIRROR = (3, 1, 2, 0)


def taps(before, centre, after):
    ends = before + after
    return [before, 0.5 * (ends + centre), 0.5 * (ends - centre), after]


def outer_weights(tables, outer):
    def chunk(r, _):
        rows = pl.ds(pl.multiple_of(r * 16, 16), 16)
        for h in range(4):
            lanes = slice(h * 128, h * 128 + 128)
            g = [tables[5 + n, rows, lanes].astype(F32) for n in range(9)]
            along_x = [taps(*g[3 * y : 3 * y + 3]) for y in range(3)]
            for c in range(4):
                along_y = taps(along_x[0][c], along_x[1][c], along_x[2][c])
                for b in range(4):
                    outer[b * 4 + c, rows, lanes] = along_y[b].astype(BF16)
        return 0

    lax.fori_loop(0, PTS // 16, chunk, 0)


def inner_weights(tables, outer, inner):
    def block(n, _):
        here = pl.ds(pl.multiple_of((n // 4) * 128, 128), 128)
        there = pl.ds(pl.multiple_of((n % 4) * 128, 128), 128)
        t = [tables[m, here, there].astype(F32) for m in range(5)]
        f = [None] + [tables[m, there, here].T.astype(F32) for m in range(1, 5)]
        above = taps(t[2], t[3], t[4])
        below = taps(f[4], f[3], f[2])
        level = taps(f[1], t[0], t[1])
        for k, (b, c) in enumerate(KEPT):
            if b == 3:
                flat = above[c]
            elif b == 1:
                flat = 0.5 * (below[c] + above[c] + level[c])
            else:
                flat = 0.5 * (below[c] + above[c] - level[c])
            ends = outer[b * 4 + c, here, there].astype(F32)
            ends = ends + outer[MIRROR[b] * 4 + MIRROR[c], there, here].T.astype(F32)
            inner[k, here, there] = (0.5 * (ends + flat)).astype(BF16)
            inner[10 + k, here, there] = (0.5 * (ends - flat)).astype(BF16)
        return 0

    lax.fori_loop(0, 16, block, 0)


def spread_line(load, store):
    along_y = []
    for px in range(2):
        d0 = load(1, px, -1)
        d1 = load(0, px, 0)
        d2 = load(1, px, 0)
        d3 = load(0, px, 1)
        along_y.append((d0 - d2, d1 + d2, d2 - d1, d1 - d3))
    for b in range(4):
        even = along_y[0][b]
        odd = along_y[1][b]
        store(b * 4 + 0, pltpu.roll(odd, 1, axis=0) - odd)
        store(b * 4 + 1, even + odd)
        store(b * 4 + 2, odd - even)
        store(b * 4 + 3, even - pltpu.roll(even, GROUP - 1, axis=0))


def spread(first, second, combine, spread_ref, base):
    def line(yp, _):
        rows = pl.ds(pl.multiple_of(yp * GROUP, GROUP), GROUP)
        for h in range(4):
            lanes = slice(h * 128, h * 128 + 128)

            def load(py, px, shift):
                near_line = jnp.clip(yp + shift, 0, LINES - 1)
                at = pl.ds(pl.multiple_of(near_line * GROUP, GROUP), GROUP)
                found = combine(
                    first[py * 2 + px, at, lanes].astype(F32), second[py * 2 + px, at, lanes].astype(F32)
                )
                if shift == 0:
                    return found
                inside = (yp + shift >= 0) & (yp + shift < LINES)
                return jnp.where(inside, found, 0.0)

            def store(n, value):
                spread_ref[base + n, rows, lanes] = value.astype(BF16)

            spread_line(load, store)
        return 0

    lax.fori_loop(0, LINES, line, 0)


def gathered_products(product, held, made):
    for b in range(4):
        for c in range(4):
            made[c] = product(b, c)
        p = [made[c] for c in range(4)]
        sides = (p[0] + p[1] + p[2], p[1] - p[2] - p[3])
        for px in range(2):
            value = sides[px]
            if b == 0:
                held[0, px] = value
            elif b == 1:
                held[0, px] += value
                held[1, px] = value
            elif b == 2:
                held[0, px] += value
                held[1, px] -= value
            else:
                held[1, px] -= value


def near_inner_kernel(low, high, tables_in, near, outer_out, parts, inner, held, made, tables, outer, sems):
    ends = pltpu.make_async_copy(tables_in.at[5:14], tables.at[5:14], sems.at[0])
    flats = pltpu.make_async_copy(tables_in.at[0:5], tables.at[0:5], sems.at[1])
    ends.start()
    flats.start()
    spread(low, high, lambda d1, d2: d1 + d2, parts, 0)
    spread(low, high, lambda d1, d2: d2 - d1, parts, 16)
    ends.wait()
    outer_weights(tables, outer)
    leaving = pltpu.make_async_copy(outer, outer_out, sems.at[2])
    leaving.start()
    flats.wait()
    inner_weights(tables, outer, inner)

    def product(a):
        def one(b, c):
            left = parts[a * 16 + b * 4 + c]
            if (b, c) in KEPT:
                return mul(left, inner[a * 10 + KEPT.index((b, c))])
            return mul_t(left, inner[a * 10 + KEPT.index((MIRROR[b], MIRROR[c]))])

        return one

    gathered_products(product(0), held, made)
    near[0] = held[...]
    near[1] = held[...]
    gathered_products(product(1), held, made)
    near[0] += held[...]
    near[1] -= held[...]
    leaving.wait()


def near_inner(low, high, tables):
    return pl.pallas_call(
        near_inner_kernel,
        name="near_inner",
        out_shape=(
            jax.ShapeDtypeStruct((2, 2, 2, ROWS, PTS), F32),
            jax.ShapeDtypeStruct((16, PTS, PTS), BF16),
        ),
        in_specs=[VMEM, VMEM, ANY],
        out_specs=(VMEM, ANY),
        scratch_shapes=[
            pltpu.VMEM((32, ROWS, PTS), BF16),
            pltpu.VMEM((20, PTS, PTS), BF16),
            pltpu.VMEM((2, 2, ROWS, PTS), F32),
            pltpu.VMEM((4, ROWS, PTS), F32),
            pltpu.VMEM((14, PTS, PTS), BF16),
            pltpu.VMEM((16, PTS, PTS), BF16),
            pltpu.SemaphoreType.DMA((3,)),
        ],
        cost_estimate=pl.CostEstimate(flops=10_000_000_000, bytes_accessed=20_000_000, transcendentals=0),
        compiler_params=pltpu.CompilerParams(vmem_limit_bytes=60 << 20),
    )(low, high, tables)


def near_outer_kernel(kept, low, high, below, above, outer_in, near_in, near, parts, held, made, outer, sems):
    weights = pltpu.make_async_copy(outer_in, outer, sems.at[0])
    inner_part = pltpu.make_async_copy(near_in, near, sems.at[1])
    weights.start()
    inner_part.start()
    spread(below, high, lambda d0, d2: d0 * kept[0] - d2, parts, 0)
    spread(low, above, lambda d1, d3: d1 - d3 * kept[1], parts, 16)
    weights.wait()
    gathered_products(
        lambda b, c: mul_t(parts[b * 4 + c], outer[MIRROR[b] * 4 + MIRROR[c]]), held, made
    )
    inner_part.wait()
    near[0] += held[...]
    gathered_products(lambda b, c: mul(parts[16 + b * 4 + c], outer[b * 4 + c]), held, made)
    near[1] -= held[...]


def near_outer(kept, low, high, below, above, outer, near):
    return pl.pallas_call(
        near_outer_kernel,
        name="near_outer",
        out_shape=jax.ShapeDtypeStruct((2, 2, 2, ROWS, PTS), F32),
        in_specs=[SMEM] + [VMEM] * 4 + [ANY] * 2,
        out_specs=VMEM,
        scratch_shapes=[
            pltpu.VMEM((32, ROWS, PTS), BF16),
            pltpu.VMEM((2, 2, ROWS, PTS), F32),
            pltpu.VMEM((4, ROWS, PTS), F32),
            pltpu.VMEM((16, PTS, PTS), BF16),
            pltpu.SemaphoreType.DMA((2,)),
        ],
        cost_estimate=pl.CostEstimate(flops=7_000_000_000, bytes_accessed=20_000_000, transcendentals=0),
        compiler_params=pltpu.CompilerParams(vmem_limit_bytes=60 << 20),
    )(kept, low, high, below, above, outer, near)


def positive_offsets(radius, minimum):
    reach = range(-radius, radius + 1)
    return [
        (z, y, x)
        for z in reach
        for y in reach
        for x in reach
        if max(abs(z), abs(y), abs(x)) >= minimum and (z, y, x) > (0, 0, 0)
    ]


RANK = {offset: row for row, offset in enumerate(positive_offsets(3, 2))}


def transfer_terms(tables, dz, reach, py, source):
    plain, flipped = ([], []), ([], [])
    blank = jnp.zeros((K, K), BF16)
    for jy in reach:
        dy = jy - py
        for jx in range(-2, 4):
            pair = []
            for px in range(2):
                offset = (dz, dy, jx - px)
                other = tuple(-d for d in offset)
                pair.append((RANK.get(offset), RANK.get(other)))
            left = None
            for way, kept in ((0, plain), (1, flipped)):
                if pair[0][way] is None and pair[1][way] is None:
                    continue
                left = source(jy, jx) if left is None else left
                kept[0].append(left)
                kept[1].append(
                    jnp.concatenate(
                        [blank if q[way] is None else tables[q[way]] for q in pair], axis=1 - way
                    )
                )
    terms = []
    if plain[0]:
        terms.append(mul(jnp.concatenate(plain[0], axis=1), jnp.concatenate(plain[1], axis=0)))
    if flipped[0]:
        terms.append(mul_t(jnp.concatenate(flipped[0], axis=1), jnp.concatenate(flipped[1], axis=1)))
    return terms


def neighbours(even, odd, count):
    return jnp.concatenate(
        [
            pltpu.roll(even, 1, axis=0),
            pltpu.roll(odd, 1, axis=0),
            even,
            odd,
            pltpu.roll(even, count - 1, axis=0),
            pltpu.roll(odd, count - 1, axis=0),
        ],
        axis=1,
    ).astype(BF16)


def coarse_lines(box, stage, slot, lines):
    stage[...] = box
    sides = []
    for py in range(2):
        halves = []
        for px in range(2):
            halves.append(
                jnp.concatenate(
                    [stage[pl.ds(32 * g + 16 * py + px, 8, stride=2), :] for g in range(6)], axis=0
                )
            )
        sides.append(halves)
    blank = jnp.zeros((8, K), F32)
    for jy in range(-2, 4):
        even, odd = sides[jy % 2]
        if jy // 2 < 0:
            even, odd = [jnp.concatenate([blank, h[: COARSE - 8]], axis=0) for h in (even, odd)]
        elif jy // 2 > 0:
            even, odd = [jnp.concatenate([h[8:], blank], axis=0) for h in (even, odd)]
        lines[slot, jy + 2] = neighbours(even, odd, COARSE)


def transfer_kernel(
    parity, kept, low, below, above, own, back2, ahead2, far3, mask, charge, merge, anterpolate, tables_in, near_in,
    potential, leaves, lines, stage, weave, flat, coarse, tables, near, fine, sems,
):
    operators = pltpu.make_async_copy(tables_in, tables, sems.at[0])
    near_part = pltpu.make_async_copy(near_in, near, sems.at[1])
    operators.start()
    near_part.start()
    packs = (below, below, low, low, above, above)
    leaves[...] = jnp.zeros_like(leaves)
    for n in range(6):
        first = PTS + (n % 2) * K
        for py in range(2):
            even = packs[n][py * 2, :, first : first + K].astype(F32)
            odd = packs[n][py * 2 + 1, :, first : first + K].astype(F32)
            if n < 2 or n > 3:
                even, odd = even * kept[n // 4], odd * kept[n // 4]
            leaves[n, py, GROUP : GROUP + ROWS, :] = neighbours(even, odd, ROWS)
    side = parity[0]
    boxes = (back2[...], merged(below, merge), own[...], merged(above, merge), ahead2[...])
    for n, (box, flag) in enumerate(zip(boxes, (2, 0, None, 1, 3))):
        box = box.astype(F32)
        coarse_lines(box if flag is None else box * kept[flag], stage, n + side, lines)
    coarse_lines(far3[...].astype(F32) * kept[4], stage, 5 - 5 * side, lines)

    operators.wait()
    for pz in range(2):

        @pl.when(side == pz)
        def _():
            for py in range(2):
                total = None
                for jz in range(-2, 4):
                    for term in transfer_terms(
                        tables,
                        jz - pz,
                        range(-2, 4),
                        py,
                        lambda jy, jx: lines[jz + 2, jy + 2, :, (jx + 2) * K : (jx + 3) * K],
                    ):
                        total = term if total is None else total + term
                coarse[py] = 0.5 * total

    for py in range(2):
        for px in range(2):
            for g in range(6):
                stage[pl.ds(32 * g + 16 * py + px, 8, stride=2), :] = coarse[
                    py, g * 8 : g * 8 + 8, px * K : px * K + K
                ]
    parent_local = stage[...].astype(BF16)

    total_charge = jnp.sum(charge[...], axis=0, keepdims=True)
    leaf_count = 2.0 * 24 * 28 * 128
    factor = wide(mask[...] * (leaf_count * PTS / total_charge))

    for py in range(2):
        for pz in range(2):
            first = (4 * pz + 2 * py) * K
            fine[pz * 2 + py] = mul_t(parent_local, merge[first : first + 2 * K, :])
        for dz in range(-3, 4):
            layers = [pz for pz in range(2) if -2 <= dz + pz <= 3]

            def source(jy, jx):
                lines_here = pl.ds(GROUP * (1 + jy // 2), ROWS)
                here = [leaves[dz + pz + 2, jy % 2, lines_here, (jx + 2) * K : (jx + 3) * K] for pz in layers]
                return jnp.concatenate(here, axis=0)

            for term in transfer_terms(tables, dz, range(-2, 4), py, source):
                for n, pz in enumerate(layers):
                    fine[pz * 2 + py] += term[n * ROWS : n * ROWS + ROWS]

    near_part.wait()
    for pz in range(2):
        for py in range(2):
            total = fine[pz * 2 + py]
            local = total.astype(BF16)
            for px in range(2):
                far = mul_t(local[:, px * K : px * K + K], anterpolate[...])
                found = (near[pz, py, px] + far) * factor
                for h in range(4):
                    flat[px, h] = found[:, h * 128 : h * 128 + 128]
                for xp in range(14):
                    for h in range(4):
                        weave[h, 2 * xp + px, pl.ds(py, LINES, stride=2), :] = flat[px, h, pl.ds(xp, LINES, stride=GROUP), :]
        for x in range(28):
            for h in range(4):
                potential[pz, x, :, h * 128 : h * 128 + 128] = weave[h, x].astype(BF16)


def transfer(parity, kept, low, below, above, own, back2, ahead2, far3, mask, charge, merge, anterpolate, tables, near):
    return pl.pallas_call(
        transfer_kernel,
        name="transfer",
        out_shape=jax.ShapeDtypeStruct((2, 28, 2 * LINES, PTS), BF16),
        in_specs=[SMEM] * 2 + [VMEM] * 11 + [ANY] * 2,
        out_specs=VMEM,
        scratch_shapes=[
            pltpu.VMEM((6, 2, ROWS + 2 * GROUP, 6 * K), BF16),
            pltpu.VMEM((6, 6, COARSE, 6 * K), BF16),
            pltpu.VMEM((ROWS, K), F32),
            pltpu.VMEM((4, 28, 2 * LINES, 128), F32),
            pltpu.VMEM((2, 4, ROWS, 128), F32),
            pltpu.VMEM((2, COARSE, 2 * K), F32),
            pltpu.VMEM((len(RANK), K, K), BF16),
            pltpu.VMEM((2, 2, 2, ROWS, PTS), F32),
            pltpu.VMEM((4, ROWS, 2 * K), F32),
            pltpu.SemaphoreType.DMA((2,)),
        ],
        cost_estimate=pl.CostEstimate(flops=12_000_000_000, bytes_accessed=20_000_000, transcendentals=0),
        compiler_params=pltpu.CompilerParams(vmem_limit_bytes=60 << 20),
    )(parity, kept, low, below, above, own, back2, ahead2, far3, mask, charge, merge, anterpolate, tables, near)


def around(count, step):
    return [(i, (i + step) % count) for i in range(count)]


def body(density, occupied, anterpolate, merge_tables, transfer_tables, near_tables):
    count = lax.axis_size("leaf")
    present = jnp.pad(occupied[0].astype(F32), ((0, 0), (0, GROUP - occupied.shape[2])))
    mask = jnp.broadcast_to(present.reshape(ROWS, 1), (ROWS, 128))
    merge = merge_tables.reshape(8 * K, K)
    low, high, own, partial = prologue(density, mask, anterpolate, merge)
    place = lax.axis_index("leaf")
    below = lax.ppermute(high, "leaf", around(count, 1))
    above = lax.ppermute(low, "leaf", around(count, -1))
    parity = place % 2
    source3 = place + 3 - 6 * parity
    kept = jnp.stack(
        [place >= 1, place < count - 1, place >= 2, place < count - 2, (source3 >= 0) & (source3 < count)]
    ).astype(F32)
    near, outer = near_inner(low, high, near_tables)
    partial, own, near = lax.optimization_barrier((partial, own, near))
    charge = lax.all_to_all(partial, "leaf", 0, 0, tiled=True)
    back2 = lax.ppermute(own, "leaf", around(count, 2))
    ahead2 = lax.ppermute(own, "leaf", around(count, -2))
    crossed = [(i, (i + 3) % count) for i in range(0, count, 2)]
    far3 = lax.ppermute(own, "leaf", crossed + [(j, i) for i, j in crossed])
    near = near_outer(kept, low, high, below, above, outer, near)
    potential = transfer(
        parity.reshape(1), kept, low, below, above, own, back2, ahead2, far3, mask, charge, merge, anterpolate,
        transfer_tables, near,
    )
    return jnp.swapaxes(potential, 1, 2)


def solution(mesh):
    return jax.shard_map(
        body,
        mesh=mesh,
        in_specs=(P("leaf", None, None, None), P("leaf", None, None), P(), P(), P(), P()),
        out_specs=P("leaf", None, None, None),
        check_vma=False,
    )
```

```python
import jax
import jax.numpy as jnp
import numpy as np
from jax import lax
from jax.experimental import pallas as pl
from jax.experimental.pallas import tpu as pltpu
from jax.sharding import PartitionSpec as P

F32 = jnp.float32
BF16 = jnp.bfloat16
GROUP = 16
LINES = 12
ROWS = GROUP * LINES
PTS = 512
K = 128
COARSE = 48
VMEM = pl.BlockSpec(memory_space=pltpu.VMEM)
SMEM = pl.BlockSpec(memory_space=pltpu.SMEM)
ANY = pl.BlockSpec(memory_space=pl.ANY)


def mul(a, b):
    return jnp.dot(a, b, preferred_element_type=F32)


def mul_t(a, b):
    return lax.dot_general(a, b, (((1,), (1,)), ((), ())), preferred_element_type=F32)


def wide(column):
    return jnp.concatenate([column] * 4, axis=1)


def prologue_kernel(density, mask, anterpolate, merge, low, high, parents, partial, stage):
    stage[...] = jnp.zeros_like(stage)
    packs = (low, high)

    def line(yp, total):
        rows = pl.ds(pl.multiple_of(yp * GROUP, GROUP), GROUP)
        present = wide(mask[rows, :])
        for z in range(2):
            for py in range(2):
                for h in range(4):
                    stage[z * 8 + py * 4 + h, 0:28, :] = density[z, 2 * yp + py, :, h * 128 : h * 128 + 128].astype(F32)
        for z in range(2):
            for py in range(2):
                for px in range(2):
                    part = jnp.concatenate(
                        [stage[z * 8 + py * 4 + h, pl.ds(px, GROUP, stride=2), :] for h in range(4)], axis=1
                    )
                    part = part * present
                    total = total + part
                    packs[z][py * 2 + px, rows, 0:PTS] = part.astype(BF16)
        return total

    total = lax.fori_loop(0, LINES, line, jnp.zeros((GROUP, PTS), F32))
    partial[...] = jnp.broadcast_to(jnp.sum(total), partial.shape)
    for z in range(2):
        found = mul(packs[z][:, :, 0:PTS].reshape(4 * ROWS, PTS), anterpolate[...]).astype(BF16)
        found = found.reshape(4, ROWS, K)
        low[:, :, PTS + z * K : PTS + z * K + K] = found
        high[:, :, PTS + z * K : PTS + z * K + K] = found
    parents[...] = merged(low, merge)


def merged(pack, merge):
    children = [pack[c % 4, :, PTS + (c // 4) * K : PTS + (c // 4) * K + K] for c in range(8)]
    return mul(jnp.concatenate(children, axis=1), merge[...]).astype(BF16)


def prologue(density, mask, anterpolate, merge):
    pack = jax.ShapeDtypeStruct((4, ROWS, PTS + 2 * K), BF16)
    return pl.pallas_call(
        prologue_kernel,
        name="prologue",
        out_shape=(
            pack,
            pack,
            jax.ShapeDtypeStruct((ROWS, K), BF16),
            jax.ShapeDtypeStruct((128, 128), F32),
        ),
        in_specs=[VMEM] * 4,
        out_specs=(VMEM,) * 4,
        scratch_shapes=[pltpu.VMEM((16, 32, 128), F32)],
        compiler_params=pltpu.CompilerParams(vmem_limit_bytes=32 << 20),
    )(density, mask, anterpolate, merge)


KEPT = [(3, 0), (3, 1), (3, 2), (3, 3), (1, 3), (2, 3), (1, 1), (1, 2), (2, 1), (2, 2)]
MIRROR = (3, 1, 2, 0)


def taps(before, centre, after):
    ends = before + after
    return [before, 0.5 * (ends + centre), 0.5 * (ends - centre), after]


def outer_weights(tables, outer):
    def chunk(r, _):
        rows = pl.ds(pl.multiple_of(r * 16, 16), 16)
        for h in range(4):
            lanes = slice(h * 128, h * 128 + 128)
            g = [tables[5 + n, rows, lanes].astype(F32) for n in range(9)]
            along_x = [taps(*g[3 * y : 3 * y + 3]) for y in range(3)]
            for c in range(4):
                along_y = taps(along_x[0][c], along_x[1][c], along_x[2][c])
                for b in range(4):
                    outer[b * 4 + c, rows, lanes] = along_y[b].astype(BF16)
        return 0

    lax.fori_loop(0, PTS // 16, chunk, 0)


def inner_weights(tables, outer, inner):
    def block(n, _):
        here = pl.ds(pl.multiple_of((n // 4) * 128, 128), 128)
        there = pl.ds(pl.multiple_of((n % 4) * 128, 128), 128)
        t = [tables[m, here, there].astype(F32) for m in range(5)]
        f = [None] + [tables[m, there, here].T.astype(F32) for m in range(1, 5)]
        above = taps(t[2], t[3], t[4])
        below = taps(f[4], f[3], f[2])
        level = taps(f[1], t[0], t[1])
        for k, (b, c) in enumerate(KEPT):
            if b == 3:
                flat = above[c]
            elif b == 1:
                flat = 0.5 * (below[c] + above[c] + level[c])
            else:
                flat = 0.5 * (below[c] + above[c] - level[c])
            ends = outer[b * 4 + c, here, there].astype(F32)
            ends = ends + outer[MIRROR[b] * 4 + MIRROR[c], there, here].T.astype(F32)
            inner[k, here, there] = (0.5 * (ends + flat)).astype(BF16)
            inner[10 + k, here, there] = (0.5 * (ends - flat)).astype(BF16)
        return 0

    lax.fori_loop(0, 16, block, 0)


def spread_line(load, store):
    along_y = []
    for px in range(2):
        d0 = load(1, px, -1)
        d1 = load(0, px, 0)
        d2 = load(1, px, 0)
        d3 = load(0, px, 1)
        along_y.append((d0 - d2, d1 + d2, d2 - d1, d1 - d3))
    for b in range(4):
        even = along_y[0][b]
        odd = along_y[1][b]
        store(b * 4 + 0, pltpu.roll(odd, 1, axis=0) - odd)
        store(b * 4 + 1, even + odd)
        store(b * 4 + 2, odd - even)
        store(b * 4 + 3, even - pltpu.roll(even, GROUP - 1, axis=0))


def spread(first, second, combine, spread_ref, base):
    def line(yp, _):
        rows = pl.ds(pl.multiple_of(yp * GROUP, GROUP), GROUP)
        for h in range(4):
            lanes = slice(h * 128, h * 128 + 128)

            def load(py, px, shift):
                near_line = jnp.clip(yp + shift, 0, LINES - 1)
                at = pl.ds(pl.multiple_of(near_line * GROUP, GROUP), GROUP)
                found = combine(
                    first[py * 2 + px, at, lanes].astype(F32), second[py * 2 + px, at, lanes].astype(F32)
                )
                if shift == 0:
                    return found
                inside = (yp + shift >= 0) & (yp + shift < LINES)
                return jnp.where(inside, found, 0.0)

            def store(n, value):
                spread_ref[base + n, rows, lanes] = value.astype(BF16)

            spread_line(load, store)
        return 0

    lax.fori_loop(0, LINES, line, 0)


def gathered_products(product, held, made):
    for b in range(4):
        for c in range(4):
            made[c] = product(b, c)
        p = [made[c] for c in range(4)]
        sides = (p[0] + p[1] + p[2], p[1] - p[2] - p[3])
        for px in range(2):
            value = sides[px]
            if b == 0:
                held[0, px] = value
            elif b == 1:
                held[0, px] += value
                held[1, px] = value
            elif b == 2:
                held[0, px] += value
                held[1, px] -= value
            else:
                held[1, px] -= value


def near_inner_kernel(low, high, tables_in, near, outer_out, parts, inner, held, made, tables, outer, sems):
    ends = pltpu.make_async_copy(tables_in.at[5:14], tables.at[5:14], sems.at[0])
    flats = pltpu.make_async_copy(tables_in.at[0:5], tables.at[0:5], sems.at[1])
    ends.start()
    flats.start()
    spread(low, high, lambda d1, d2: d1 + d2, parts, 0)
    spread(low, high, lambda d1, d2: d2 - d1, parts, 16)
    ends.wait()
    outer_weights(tables, outer)
    leaving = pltpu.make_async_copy(outer, outer_out, sems.at[2])
    leaving.start()
    flats.wait()
    inner_weights(tables, outer, inner)

    def product(a):
        def one(b, c):
            left = parts[a * 16 + b * 4 + c]
            if (b, c) in KEPT:
                return mul(left, inner[a * 10 + KEPT.index((b, c))])
            return mul_t(left, inner[a * 10 + KEPT.index((MIRROR[b], MIRROR[c]))])

        return one

    gathered_products(product(0), held, made)
    near[0] = held[...]
    near[1] = held[...]
    gathered_products(product(1), held, made)
    near[0] += held[...]
    near[1] -= held[...]
    leaving.wait()


def near_inner(low, high, tables):
    return pl.pallas_call(
        near_inner_kernel,
        name="near_inner",
        out_shape=(
            jax.ShapeDtypeStruct((2, 2, 2, ROWS, PTS), F32),
            jax.ShapeDtypeStruct((16, PTS, PTS), BF16),
        ),
        in_specs=[VMEM, VMEM, ANY],
        out_specs=(VMEM, ANY),
        scratch_shapes=[
            pltpu.VMEM((32, ROWS, PTS), BF16),
            pltpu.VMEM((20, PTS, PTS), BF16),
            pltpu.VMEM((2, 2, ROWS, PTS), F32),
            pltpu.VMEM((4, ROWS, PTS), F32),
            pltpu.VMEM((14, PTS, PTS), BF16),
            pltpu.VMEM((16, PTS, PTS), BF16),
            pltpu.SemaphoreType.DMA((3,)),
        ],
        cost_estimate=pl.CostEstimate(flops=10_000_000_000, bytes_accessed=20_000_000, transcendentals=0),
        compiler_params=pltpu.CompilerParams(vmem_limit_bytes=60 << 20),
    )(low, high, tables)


def near_outer_kernel(kept, low, high, below, above, outer_in, near_in, near, parts, held, made, outer, sems):
    weights = pltpu.make_async_copy(outer_in, outer, sems.at[0])
    inner_part = pltpu.make_async_copy(near_in, near, sems.at[1])
    weights.start()
    inner_part.start()
    spread(below, high, lambda d0, d2: d0 * kept[0] - d2, parts, 0)
    spread(low, above, lambda d1, d3: d1 - d3 * kept[1], parts, 16)
    weights.wait()
    gathered_products(
        lambda b, c: mul_t(parts[b * 4 + c], outer[MIRROR[b] * 4 + MIRROR[c]]), held, made
    )
    inner_part.wait()
    near[0] += held[...]
    gathered_products(lambda b, c: mul(parts[16 + b * 4 + c], outer[b * 4 + c]), held, made)
    near[1] -= held[...]


def near_outer(kept, low, high, below, above, outer, near):
    return pl.pallas_call(
        near_outer_kernel,
        name="near_outer",
        out_shape=jax.ShapeDtypeStruct((2, 2, 2, ROWS, PTS), F32),
        in_specs=[SMEM] + [VMEM] * 4 + [ANY] * 2,
        out_specs=VMEM,
        scratch_shapes=[
            pltpu.VMEM((32, ROWS, PTS), BF16),
            pltpu.VMEM((2, 2, ROWS, PTS), F32),
            pltpu.VMEM((4, ROWS, PTS), F32),
            pltpu.VMEM((16, PTS, PTS), BF16),
            pltpu.SemaphoreType.DMA((2,)),
        ],
        cost_estimate=pl.CostEstimate(flops=7_000_000_000, bytes_accessed=20_000_000, transcendentals=0),
        compiler_params=pltpu.CompilerParams(vmem_limit_bytes=60 << 20),
    )(kept, low, high, below, above, outer, near)


def positive_offsets(radius, minimum):
    reach = range(-radius, radius + 1)
    return [
        (z, y, x)
        for z in reach
        for y in reach
        for x in reach
        if max(abs(z), abs(y), abs(x)) >= minimum and (z, y, x) > (0, 0, 0)
    ]


RANK = {offset: row for row, offset in enumerate(positive_offsets(3, 2))}


def transfer_terms(tables, dz, reach, py, source):
    plain, flipped = ([], []), ([], [])
    blank = jnp.zeros((K, K), BF16)
    for jy in reach:
        dy = jy - py
        for jx in range(-2, 4):
            pair = []
            for px in range(2):
                offset = (dz, dy, jx - px)
                other = tuple(-d for d in offset)
                pair.append((RANK.get(offset), RANK.get(other)))
            left = None
            for way, kept in ((0, plain), (1, flipped)):
                if pair[0][way] is None and pair[1][way] is None:
                    continue
                left = source(jy, jx) if left is None else left
                kept[0].append(left)
                kept[1].append(
                    jnp.concatenate(
                        [blank if q[way] is None else tables[q[way]] for q in pair], axis=1 - way
                    )
                )
    terms = []
    if plain[0]:
        terms.append(mul(jnp.concatenate(plain[0], axis=1), jnp.concatenate(plain[1], axis=0)))
    if flipped[0]:
        terms.append(mul_t(jnp.concatenate(flipped[0], axis=1), jnp.concatenate(flipped[1], axis=1)))
    return terms


def neighbours(even, odd, count):
    return jnp.concatenate(
        [
            pltpu.roll(even, 1, axis=0),
            pltpu.roll(odd, 1, axis=0),
            even,
            odd,
            pltpu.roll(even, count - 1, axis=0),
            pltpu.roll(odd, count - 1, axis=0),
        ],
        axis=1,
    ).astype(BF16)


def coarse_lines(box, stage, slot, lines):
    stage[...] = box
    sides = []
    for py in range(2):
        halves = []
        for px in range(2):
            halves.append(
                jnp.concatenate(
                    [stage[pl.ds(32 * g + 16 * py + px, 8, stride=2), :] for g in range(6)], axis=0
                )
            )
        sides.append(halves)
    blank = jnp.zeros((8, K), F32)
    for jy in range(-2, 4):
        even, odd = sides[jy % 2]
        if jy // 2 < 0:
            even, odd = [jnp.concatenate([blank, h[: COARSE - 8]], axis=0) for h in (even, odd)]
        elif jy // 2 > 0:
            even, odd = [jnp.concatenate([h[8:], blank], axis=0) for h in (even, odd)]
        lines[slot, jy + 2] = neighbours(even, odd, COARSE)


def transfer_kernel(
    parity, kept, low, below, above, own, back2, ahead2, far3, mask, charge, merge, anterpolate, tables_in, near_in,
    potential, leaves, lines, stage, weave, flat, coarse, tables, near, fine, sems,
):
    operators = pltpu.make_async_copy(tables_in, tables, sems.at[0])
    near_part = pltpu.make_async_copy(near_in, near, sems.at[1])
    operators.start()
    near_part.start()
    packs = (below, below, low, low, above, above)
    leaves[...] = jnp.zeros_like(leaves)
    for n in range(6):
        first = PTS + (n % 2) * K
        for py in range(2):
            even = packs[n][py * 2, :, first : first + K].astype(F32)
            odd = packs[n][py * 2 + 1, :, first : first + K].astype(F32)
            if n < 2 or n > 3:
                even, odd = even * kept[n // 4], odd * kept[n // 4]
            leaves[n, py, GROUP : GROUP + ROWS, :] = neighbours(even, odd, ROWS)
    side = parity[0]
    boxes = (back2[...], merged(below, merge), own[...], merged(above, merge), ahead2[...])
    for n, (box, flag) in enumerate(zip(boxes, (2, 0, None, 1, 3))):
        box = box.astype(F32)
        coarse_lines(box if flag is None else box * kept[flag], stage, n + side, lines)
    coarse_lines(far3[...].astype(F32) * kept[4], stage, 5 - 5 * side, lines)

    operators.wait()
    coarse[...] = jnp.zeros_like(coarse)
    fine[...] = jnp.zeros_like(fine)
    for py in range(2):
        for dz in range(-3, 4):
            layers = [pz for pz in range(2) if -2 <= dz + pz <= 3]
            slot = jnp.clip(dz + side + 2, 0, 5)

            def source(jy, jx):
                lines_here = pl.ds(GROUP * (1 + jy // 2), ROWS)
                lanes = slice((jx + 2) * K, (jx + 3) * K)
                here = [leaves[dz + pz + 2, jy % 2, lines_here, lanes] for pz in layers]
                return jnp.concatenate(here + [lines[slot, jy + 2, :, lanes]], axis=0)

            for term in transfer_terms(tables, dz, range(-2, 4), py, source):
                for n, pz in enumerate(layers):
                    fine[pz * 2 + py] += term[n * ROWS : n * ROWS + ROWS]
                wider = term[len(layers) * ROWS :]
                if abs(dz) == 3:
                    wider = jnp.where(side == (dz < 0), wider, 0.0)
                coarse[py] += 0.5 * wider

    for py in range(2):
        for px in range(2):
            for g in range(6):
                stage[pl.ds(32 * g + 16 * py + px, 8, stride=2), :] = coarse[
                    py, g * 8 : g * 8 + 8, px * K : px * K + K
                ]
    parent_local = stage[...].astype(BF16)

    total_charge = jnp.sum(charge[...], axis=0, keepdims=True)
    leaf_count = 2.0 * 24 * 28 * 128
    factor = wide(mask[...] * (leaf_count * PTS / total_charge))

    near_part.wait()
    for pz in range(2):
        for py in range(2):
            first = (4 * pz + 2 * py) * K
            total = fine[pz * 2 + py] + mul_t(parent_local, merge[first : first + 2 * K, :])
            local = total.astype(BF16)
            for px in range(2):
                far = mul_t(local[:, px * K : px * K + K], anterpolate[...])
                found = (near[pz, py, px] + far) * factor
                for h in range(4):
                    flat[px, h] = found[:, h * 128 : h * 128 + 128]
                for xp in range(14):
                    for h in range(4):
                        weave[h, 2 * xp + px, pl.ds(py, LINES, stride=2), :] = flat[px, h, pl.ds(xp, LINES, stride=GROUP), :]
        for x in range(28):
            for h in range(4):
                potential[pz, x, :, h * 128 : h * 128 + 128] = weave[h, x].astype(BF16)


def transfer(parity, kept, low, below, above, own, back2, ahead2, far3, mask, charge, merge, anterpolate, tables, near):
    return pl.pallas_call(
        transfer_kernel,
        name="transfer",
        out_shape=jax.ShapeDtypeStruct((2, 28, 2 * LINES, PTS), BF16),
        in_specs=[SMEM] * 2 + [VMEM] * 11 + [ANY] * 2,
        out_specs=VMEM,
        scratch_shapes=[
            pltpu.VMEM((6, 2, ROWS + 2 * GROUP, 6 * K), BF16),
            pltpu.VMEM((6, 6, COARSE, 6 * K), BF16),
            pltpu.VMEM((ROWS, K), F32),
            pltpu.VMEM((4, 28, 2 * LINES, 128), F32),
            pltpu.VMEM((2, 4, ROWS, 128), F32),
            pltpu.VMEM((2, COARSE, 2 * K), F32),
            pltpu.VMEM((len(RANK), K, K), BF16),
            pltpu.VMEM((2, 2, 2, ROWS, PTS), F32),
            pltpu.VMEM((4, ROWS, 2 * K), F32),
            pltpu.SemaphoreType.DMA((2,)),
        ],
        cost_estimate=pl.CostEstimate(flops=12_000_000_000, bytes_accessed=20_000_000, transcendentals=0),
        compiler_params=pltpu.CompilerParams(vmem_limit_bytes=60 << 20),
    )(parity, kept, low, below, above, own, back2, ahead2, far3, mask, charge, merge, anterpolate, tables, near)


def around(count, step):
    return [(i, (i + step) % count) for i in range(count)]


def body(density, occupied, anterpolate, merge_tables, transfer_tables, near_tables):
    count = lax.axis_size("leaf")
    present = jnp.pad(occupied[0].astype(F32), ((0, 0), (0, GROUP - occupied.shape[2])))
    mask = jnp.broadcast_to(present.reshape(ROWS, 1), (ROWS, 128))
    merge = merge_tables.reshape(8 * K, K)
    low, high, own, partial = prologue(density, mask, anterpolate, merge)
    place = lax.axis_index("leaf")
    below = lax.ppermute(high, "leaf", around(count, 1))
    above = lax.ppermute(low, "leaf", around(count, -1))
    charge = lax.all_to_all(partial, "leaf", 0, 0, tiled=True)
    parity = place % 2
    source3 = place + 3 - 6 * parity
    kept = jnp.stack(
        [place >= 1, place < count - 1, place >= 2, place < count - 2, (source3 >= 0) & (source3 < count)]
    ).astype(F32)
    near, outer = near_inner(low, high, near_tables)
    own, near = lax.optimization_barrier((own, near))
    back2 = lax.ppermute(own, "leaf", around(count, 2))
    ahead2 = lax.ppermute(own, "leaf", around(count, -2))
    crossed = [(i, (i + 3) % count) for i in range(0, count, 2)]
    far3 = lax.ppermute(own, "leaf", crossed + [(j, i) for i, j in crossed])
    near = near_outer(kept, low, high, below, above, outer, near)
    potential = transfer(
        parity.reshape(1), kept, low, below, above, own, back2, ahead2, far3, mask, charge, merge, anterpolate,
        transfer_tables, near,
    )
    return jnp.swapaxes(potential, 1, 2)


def solution(mesh):
    return jax.shard_map(
        body,
        mesh=mesh,
        in_specs=(P("leaf", None, None, None), P("leaf", None, None), P(), P(), P(), P()),
        out_specs=P("leaf", None, None, None),
        check_vma=False,
    )
```

```python
import functools

import jax
import jax.numpy as jnp
from jax import lax
from jax.experimental import pallas as pl
from jax.experimental.pallas import tpu as pltpu
from jax.sharding import PartitionSpec as P

F32 = jnp.float32
BF16 = jnp.bfloat16
GROUP = 16
LINES = 12
ROWS = GROUP * LINES
PTS = 512
K = 128
COARSE = 48
VMEM = pl.BlockSpec(memory_space=pltpu.VMEM)
SMEM = pl.BlockSpec(memory_space=pltpu.SMEM)
ANY = pl.BlockSpec(memory_space=pl.ANY)


def mul(a, b):
    return jnp.dot(a, b, preferred_element_type=F32)


def mul_t(a, b):
    return lax.dot_general(a, b, (((1,), (1,)), ((), ())), preferred_element_type=F32)


def wide(column):
    return jnp.concatenate([column] * 4, axis=1)


def prologue_kernel(density, mask, anterpolate, merge, low, high, parents, partial, stage):
    stage[...] = jnp.zeros_like(stage)
    packs = (low, high)

    def line(yp, total):
        rows = pl.ds(pl.multiple_of(yp * GROUP, GROUP), GROUP)
        present = wide(mask[rows, :])
        for z in range(2):
            for py in range(2):
                for h in range(4):
                    stage[z * 8 + py * 4 + h, 0:28, :] = density[z, 2 * yp + py, :, h * 128 : h * 128 + 128].astype(F32)
        for z in range(2):
            for py in range(2):
                for px in range(2):
                    part = jnp.concatenate(
                        [stage[z * 8 + py * 4 + h, pl.ds(px, GROUP, stride=2), :] for h in range(4)], axis=1
                    )
                    part = part * present
                    total = total + part
                    packs[z][py * 2 + px, rows, 0:PTS] = part.astype(BF16)
        return total

    total = lax.fori_loop(0, LINES, line, jnp.zeros((GROUP, PTS), F32), unroll=4)
    partial[...] = jnp.broadcast_to(jnp.sum(total), partial.shape)
    for z in range(2):
        found = mul(packs[z][:, :, 0:PTS].reshape(4 * ROWS, PTS), anterpolate[...]).astype(BF16)
        found = found.reshape(4, ROWS, K)
        low[:, :, PTS + z * K : PTS + z * K + K] = found
        high[:, :, PTS + z * K : PTS + z * K + K] = found
    parents[...] = merged(low, merge)


def merged(pack, merge):
    children = [pack[c % 4, :, PTS + (c // 4) * K : PTS + (c // 4) * K + K] for c in range(8)]
    return mul(jnp.concatenate(children, axis=1), merge[...]).astype(BF16)


def prologue(density, mask, anterpolate, merge):
    pack = jax.ShapeDtypeStruct((4, ROWS, PTS + 2 * K), BF16)
    return pl.pallas_call(
        prologue_kernel,
        name="prologue",
        out_shape=(
            pack,
            pack,
            jax.ShapeDtypeStruct((ROWS, K), BF16),
            jax.ShapeDtypeStruct((128, 128), F32),
        ),
        in_specs=[VMEM] * 4,
        out_specs=(VMEM,) * 4,
        scratch_shapes=[pltpu.VMEM((16, 32, 128), F32)],
        compiler_params=pltpu.CompilerParams(vmem_limit_bytes=32 << 20),
    )(density, mask, anterpolate, merge)


KEPT = [(3, 0), (3, 1), (3, 2), (3, 3), (1, 3), (2, 3), (1, 1), (1, 2), (2, 1), (2, 2)]
MIRROR = (3, 1, 2, 0)


def taps(before, centre, after):
    ends = before + after
    return [before, 0.5 * (ends + centre), 0.5 * (ends - centre), after]


def outer_weights(tables, outer):
    def chunk(r, _):
        rows = pl.ds(pl.multiple_of(r * 16, 16), 16)
        for h in range(4):
            lanes = slice(h * 128, h * 128 + 128)
            g = [tables[5 + n, rows, lanes].astype(F32) for n in range(9)]
            along_x = [taps(*g[3 * y : 3 * y + 3]) for y in range(3)]
            for c in range(4):
                along_y = taps(along_x[0][c], along_x[1][c], along_x[2][c])
                for b in range(4):
                    outer[b * 4 + c, rows, lanes] = along_y[b].astype(BF16)
        return 0

    lax.fori_loop(0, PTS // 16, chunk, 0, unroll=4)


def inner_weights(tables, outer, inner):
    def block(n, _):
        here = pl.ds(pl.multiple_of((n // 4) * 128, 128), 128)
        there = pl.ds(pl.multiple_of((n % 4) * 128, 128), 128)
        t = [tables[m, here, there].astype(F32) for m in range(5)]
        f = [None] + [tables[m, there, here].T.astype(F32) for m in range(1, 5)]
        above = taps(t[2], t[3], t[4])
        below = taps(f[4], f[3], f[2])
        level = taps(f[1], t[0], t[1])
        for k, (b, c) in enumerate(KEPT):
            if b == 3:
                flat = above[c]
            elif b == 1:
                flat = 0.5 * (below[c] + above[c] + level[c])
            else:
                flat = 0.5 * (below[c] + above[c] - level[c])
            ends = outer[b * 4 + c, here, there].astype(F32)
            ends = ends + outer[MIRROR[b] * 4 + MIRROR[c], there, here].T.astype(F32)
            inner[k, here, there] = (0.5 * (ends + flat)).astype(BF16)
            inner[10 + k, here, there] = (0.5 * (ends - flat)).astype(BF16)
        return 0

    lax.fori_loop(0, 16, block, 0, unroll=4)


def spread_line(load, store):
    along_y = []
    for px in range(2):
        d0 = load(1, px, -1)
        d1 = load(0, px, 0)
        d2 = load(1, px, 0)
        d3 = load(0, px, 1)
        along_y.append((d0 - d2, d1 + d2, d2 - d1, d1 - d3))
    for b in range(4):
        even = along_y[0][b]
        odd = along_y[1][b]
        store(b * 4 + 0, pltpu.roll(odd, 1, axis=0) - odd)
        store(b * 4 + 1, even + odd)
        store(b * 4 + 2, odd - even)
        store(b * 4 + 3, even - pltpu.roll(even, GROUP - 1, axis=0))


def spread(first, second, combine, spread_ref, base):
    def line(yp, _):
        rows = pl.ds(pl.multiple_of(yp * GROUP, GROUP), GROUP)
        for h in range(4):
            lanes = slice(h * 128, h * 128 + 128)

            def load(py, px, shift):
                near_line = jnp.clip(yp + shift, 0, LINES - 1)
                at = pl.ds(pl.multiple_of(near_line * GROUP, GROUP), GROUP)
                found = combine(
                    first[py * 2 + px, at, lanes].astype(F32), second[py * 2 + px, at, lanes].astype(F32)
                )
                if shift == 0:
                    return found
                inside = (yp + shift >= 0) & (yp + shift < LINES)
                return jnp.where(inside, found, 0.0)

            def store(n, value):
                spread_ref[base + n, rows, lanes] = value.astype(BF16)

            spread_line(load, store)
        return 0

    lax.fori_loop(0, LINES, line, 0, unroll=4)


def gathered_products(product, held, made):
    for b in range(4):
        for c in range(4):
            made[4 * b + c] = product(b, c)
        p = [made[4 * b + c] for c in range(4)]
        sides = (p[0] + p[1] + p[2], p[1] - p[2] - p[3])
        for px in range(2):
            value = sides[px]
            if b == 0:
                held[0, px] = value
            elif b == 1:
                held[0, px] += value
                held[1, px] = value
            elif b == 2:
                held[0, px] += value
                held[1, px] -= value
            else:
                held[1, px] -= value


def near_inner_kernel(low, high, tables_in, near, outer_out, parts, inner, held, made, tables, outer, sems):
    ends = pltpu.make_async_copy(tables_in.at[5:14], tables.at[5:14], sems.at[0])
    flats = pltpu.make_async_copy(tables_in.at[0:5], tables.at[0:5], sems.at[1])
    ends.start()
    flats.start()
    spread(low, high, lambda d1, d2: d1 + d2, parts, 0)
    spread(low, high, lambda d1, d2: d2 - d1, parts, 16)
    ends.wait()
    outer_weights(tables, outer)
    leaving = pltpu.make_async_copy(outer, outer_out, sems.at[2])
    leaving.start()
    flats.wait()
    inner_weights(tables, outer, inner)

    def product(a):
        def one(b, c):
            left = parts[a * 16 + b * 4 + c]
            if (b, c) in KEPT:
                return mul(left, inner[a * 10 + KEPT.index((b, c))])
            return mul_t(left, inner[a * 10 + KEPT.index((MIRROR[b], MIRROR[c]))])

        return one

    for a in range(2):
        gathered_products(product(a), held.at[a], made)
    near[0] = held[0] + held[1]
    near[1] = held[0] - held[1]
    leaving.wait()


def near_inner(low, high, tables):
    return pl.pallas_call(
        near_inner_kernel,
        name="near_inner",
        out_shape=(
            jax.ShapeDtypeStruct((2, 2, 2, ROWS, PTS), F32),
            jax.ShapeDtypeStruct((16, PTS, PTS), BF16),
        ),
        in_specs=[VMEM, VMEM, ANY],
        out_specs=(VMEM, ANY),
        scratch_shapes=[
            pltpu.VMEM((32, ROWS, PTS), BF16),
            pltpu.VMEM((20, PTS, PTS), BF16),
            pltpu.VMEM((2, 2, 2, ROWS, PTS), F32),
            pltpu.VMEM((16, ROWS, PTS), F32),
            pltpu.VMEM((14, PTS, PTS), BF16),
            pltpu.VMEM((16, PTS, PTS), BF16),
            pltpu.SemaphoreType.DMA((3,)),
        ],
        cost_estimate=pl.CostEstimate(flops=10_000_000_000, bytes_accessed=20_000_000, transcendentals=0),
        compiler_params=pltpu.CompilerParams(vmem_limit_bytes=60 << 20),
    )(low, high, tables)


def flags(place, count):
    third = place + 3 - 6 * (place % 2)
    found = (place >= 1, place < count - 1, place >= 2, place < count - 2, (third >= 0) & (third < count))
    return [jnp.where(f, 1.0, 0.0) for f in found]


def near_outer_kernel(count, place, low, high, below, above, outer_in, near_in, near, parts, held, made, outer, sems):
    kept = flags(place[0], count)
    weights = pltpu.make_async_copy(outer_in, outer, sems.at[0])
    inner_part = pltpu.make_async_copy(near_in, near, sems.at[1])
    weights.start()
    inner_part.start()
    spread(below, high, lambda d0, d2: d0 * kept[0] - d2, parts, 0)
    spread(low, above, lambda d1, d3: d1 - d3 * kept[1], parts, 16)
    weights.wait()
    gathered_products(
        lambda b, c: mul_t(parts[b * 4 + c], outer[MIRROR[b] * 4 + MIRROR[c]]), held, made
    )
    inner_part.wait()
    near[0] += held[...]
    gathered_products(lambda b, c: mul(parts[16 + b * 4 + c], outer[b * 4 + c]), held, made)
    near[1] -= held[...]


def near_outer(count, place, low, high, below, above, outer, near):
    return pl.pallas_call(
        functools.partial(near_outer_kernel, count),
        name="near_outer",
        out_shape=jax.ShapeDtypeStruct((2, 2, 2, ROWS, PTS), F32),
        in_specs=[SMEM] + [VMEM] * 4 + [ANY] * 2,
        out_specs=VMEM,
        scratch_shapes=[
            pltpu.VMEM((32, ROWS, PTS), BF16),
            pltpu.VMEM((2, 2, ROWS, PTS), F32),
            pltpu.VMEM((16, ROWS, PTS), F32),
            pltpu.VMEM((16, PTS, PTS), BF16),
            pltpu.SemaphoreType.DMA((2,)),
        ],
        cost_estimate=pl.CostEstimate(flops=7_000_000_000, bytes_accessed=20_000_000, transcendentals=0),
        compiler_params=pltpu.CompilerParams(vmem_limit_bytes=60 << 20),
    )(place, low, high, below, above, outer, near)


def positive_offsets(radius, minimum):
    reach = range(-radius, radius + 1)
    return [
        (z, y, x)
        for z in reach
        for y in reach
        for x in reach
        if max(abs(z), abs(y), abs(x)) >= minimum and (z, y, x) > (0, 0, 0)
    ]


RANK = {offset: row for row, offset in enumerate(positive_offsets(3, 2))}


def transfer_terms(tables, dz, reach, py, source):
    plain, flipped = ([], []), ([], [])
    blank = jnp.zeros((K, K), BF16)
    for jy in reach:
        dy = jy - py
        for jx in range(-2, 4):
            pair = []
            for px in range(2):
                offset = (dz, dy, jx - px)
                other = tuple(-d for d in offset)
                pair.append((RANK.get(offset), RANK.get(other)))
            left = None
            for way, kept in ((0, plain), (1, flipped)):
                if pair[0][way] is None and pair[1][way] is None:
                    continue
                left = source(jy, jx) if left is None else left
                kept[0].append(left)
                kept[1].append(
                    jnp.concatenate(
                        [blank if q[way] is None else tables[q[way]] for q in pair], axis=1 - way
                    )
                )
    terms = []
    if plain[0]:
        terms.append(mul(jnp.concatenate(plain[0], axis=1), jnp.concatenate(plain[1], axis=0)))
    if flipped[0]:
        terms.append(mul_t(jnp.concatenate(flipped[0], axis=1), jnp.concatenate(flipped[1], axis=1)))
    return terms


def neighbours(even, odd, count):
    return jnp.concatenate(
        [
            pltpu.roll(even, 1, axis=0),
            pltpu.roll(odd, 1, axis=0),
            even,
            odd,
            pltpu.roll(even, count - 1, axis=0),
            pltpu.roll(odd, count - 1, axis=0),
        ],
        axis=1,
    ).astype(BF16)


def coarse_lines(box, stage, slot, lines):
    stage[...] = box
    sides = []
    for py in range(2):
        halves = []
        for px in range(2):
            halves.append(
                jnp.concatenate(
                    [stage[pl.ds(32 * g + 16 * py + px, 8, stride=2), :] for g in range(6)], axis=0
                )
            )
        sides.append(halves)
    blank = jnp.zeros((8, K), F32)
    for jy in range(-2, 4):
        even, odd = sides[jy % 2]
        if jy // 2 < 0:
            even, odd = [jnp.concatenate([blank, h[: COARSE - 8]], axis=0) for h in (even, odd)]
        elif jy // 2 > 0:
            even, odd = [jnp.concatenate([h[8:], blank], axis=0) for h in (even, odd)]
        lines[slot, jy + 2] = neighbours(even, odd, COARSE)


def transfer_kernel(
    count, place, low, below, above, own, back2, ahead2, far3, mask, charge, merge, anterpolate, tables_in, near_in,
    potential, leaves, lines, stage, weave, flat, coarse, tables, near, fine, sems,
):
    kept = flags(place[0], count)
    operators = pltpu.make_async_copy(tables_in, tables, sems.at[0])
    near_part = pltpu.make_async_copy(near_in, near, sems.at[1])
    operators.start()
    near_part.start()
    packs = (below, below, low, low, above, above)
    leaves[...] = jnp.zeros_like(leaves)
    for n in range(6):
        first = PTS + (n % 2) * K
        for py in range(2):
            even = packs[n][py * 2, :, first : first + K].astype(F32)
            odd = packs[n][py * 2 + 1, :, first : first + K].astype(F32)
            if n < 2 or n > 3:
                even, odd = even * kept[n // 4], odd * kept[n // 4]
            leaves[n, py, GROUP : GROUP + ROWS, :] = neighbours(even, odd, ROWS)
    side = place[0] % 2
    boxes = (back2[...], merged(below, merge), own[...], merged(above, merge), ahead2[...])
    for n, (box, flag) in enumerate(zip(boxes, (2, 0, None, 1, 3))):
        box = box.astype(F32)
        coarse_lines(box if flag is None else box * kept[flag], stage, n + side, lines)
    coarse_lines(far3[...].astype(F32) * kept[4], stage, 5 - 5 * side, lines)

    operators.wait()
    coarse[...] = jnp.zeros_like(coarse)
    fine[...] = jnp.zeros_like(fine)
    for py in range(2):
        for dz in range(-3, 4):
            layers = [pz for pz in range(2) if -2 <= dz + pz <= 3]
            slot = jnp.clip(dz + side + 2, 0, 5)

            def source(jy, jx):
                lines_here = pl.ds(GROUP * (1 + jy // 2), ROWS)
                lanes = slice((jx + 2) * K, (jx + 3) * K)
                here = [leaves[dz + pz + 2, jy % 2, lines_here, lanes] for pz in layers]
                return jnp.concatenate(here + [lines[slot, jy + 2, :, lanes]], axis=0)

            for term in transfer_terms(tables, dz, range(-2, 4), py, source):
                for n, pz in enumerate(layers):
                    fine[pz * 2 + py] += term[n * ROWS : n * ROWS + ROWS]
                wider = term[len(layers) * ROWS :]
                if abs(dz) == 3:
                    wider = jnp.where(side == (dz < 0), wider, 0.0)
                coarse[py] += 0.5 * wider

    for py in range(2):
        for px in range(2):
            for g in range(6):
                stage[pl.ds(32 * g + 16 * py + px, 8, stride=2), :] = coarse[
                    py, g * 8 : g * 8 + 8, px * K : px * K + K
                ]
    parent_local = stage[...].astype(BF16)

    total_charge = jnp.sum(charge[...], axis=0, keepdims=True)
    leaf_count = 2.0 * 24 * 28 * 128
    factor = wide(mask[...] * (leaf_count * PTS / total_charge))

    near_part.wait()
    for pz in range(2):
        for py in range(2):
            first = (4 * pz + 2 * py) * K
            total = fine[pz * 2 + py] + mul_t(parent_local, merge[first : first + 2 * K, :])
            local = total.astype(BF16)
            for px in range(2):
                far = mul_t(local[:, px * K : px * K + K], anterpolate[...])
                found = (near[pz, py, px] + far) * factor
                for h in range(4):
                    flat[px, h] = found[:, h * 128 : h * 128 + 128]
                for xp in range(14):
                    for h in range(4):
                        weave[h, 2 * xp + px, pl.ds(py, LINES, stride=2), :] = flat[px, h, pl.ds(xp, LINES, stride=GROUP), :]
        for x in range(28):
            for h in range(4):
                potential[pz, x, :, h * 128 : h * 128 + 128] = weave[h, x].astype(BF16)


def transfer(count, place, low, below, above, own, back2, ahead2, far3, mask, charge, merge, anterpolate, tables, near):
    return pl.pallas_call(
        functools.partial(transfer_kernel, count),
        name="transfer",
        out_shape=jax.ShapeDtypeStruct((2, 28, 2 * LINES, PTS), BF16),
        in_specs=[SMEM] + [VMEM] * 11 + [ANY] * 2,
        out_specs=VMEM,
        scratch_shapes=[
            pltpu.VMEM((6, 2, ROWS + 2 * GROUP, 6 * K), BF16),
            pltpu.VMEM((6, 6, COARSE, 6 * K), BF16),
            pltpu.VMEM((ROWS, K), F32),
            pltpu.VMEM((4, 28, 2 * LINES, 128), F32),
            pltpu.VMEM((2, 4, ROWS, 128), F32),
            pltpu.VMEM((2, COARSE, 2 * K), F32),
            pltpu.VMEM((len(RANK), K, K), BF16),
            pltpu.VMEM((2, 2, 2, ROWS, PTS), F32),
            pltpu.VMEM((4, ROWS, 2 * K), F32),
            pltpu.SemaphoreType.DMA((2,)),
        ],
        cost_estimate=pl.CostEstimate(flops=12_000_000_000, bytes_accessed=20_000_000, transcendentals=0),
        compiler_params=pltpu.CompilerParams(vmem_limit_bytes=60 << 20),
    )(place, low, below, above, own, back2, ahead2, far3, mask, charge, merge, anterpolate, tables, near)


def around(count, step):
    return [(i, (i + step) % count) for i in range(count)]


def body(density, occupied, anterpolate, merge_tables, transfer_tables, near_tables):
    count = lax.axis_size("leaf")
    present = jnp.pad(occupied[0].astype(F32), ((0, 0), (0, GROUP - occupied.shape[2])))
    mask = jnp.broadcast_to(present.reshape(ROWS, 1), (ROWS, 128))
    merge = merge_tables.reshape(8 * K, K)
    low, high, own, partial = prologue(density, mask, anterpolate, merge)
    place = lax.axis_index("leaf").reshape(1)
    below = lax.ppermute(high, "leaf", around(count, 1))
    above = lax.ppermute(low, "leaf", around(count, -1))
    charge = lax.all_to_all(partial, "leaf", 0, 0, tiled=True)
    near, outer = near_inner(low, high, near_tables)
    own, near = lax.optimization_barrier((own, near))
    back2 = lax.ppermute(own, "leaf", around(count, 2))
    ahead2 = lax.ppermute(own, "leaf", around(count, -2))
    crossed = [(i, (i + 3) % count) for i in range(0, count, 2)]
    far3 = lax.ppermute(own, "leaf", crossed + [(j, i) for i, j in crossed])
    near = near_outer(count, place, low, high, below, above, outer, near)
    potential = transfer(
        count, place, low, below, above, own, back2, ahead2, far3, mask, charge, merge, anterpolate,
        transfer_tables, near,
    )
    return jnp.swapaxes(potential, 1, 2)


def solution(mesh):
    return jax.shard_map(
        body,
        mesh=mesh,
        in_specs=(P("leaf", None, None, None), P("leaf", None, None), P(), P(), P(), P()),
        out_specs=P("leaf", None, None, None),
        check_vma=False,
    )
```

```python
import functools

import jax
import jax.numpy as jnp
from jax import lax
from jax.experimental import pallas as pl
from jax.experimental.pallas import tpu as pltpu
from jax.sharding import PartitionSpec as P

F32 = jnp.float32
BF16 = jnp.bfloat16
GROUP = 16
LINES = 12
ROWS = GROUP * LINES
PTS = 512
K = 128
COARSE = 48
VMEM = pl.BlockSpec(memory_space=pltpu.VMEM)
SMEM = pl.BlockSpec(memory_space=pltpu.SMEM)
ANY = pl.BlockSpec(memory_space=pl.ANY)


def mul(a, b):
    return jnp.dot(a, b, preferred_element_type=F32)


def mul_t(a, b):
    return lax.dot_general(a, b, (((1,), (1,)), ((), ())), preferred_element_type=F32)


def wide(column):
    return jnp.concatenate([column] * 4, axis=1)


def prologue_kernel(density, mask, anterpolate, merge, low, high, parents, partial, stage):
    stage[...] = jnp.zeros_like(stage)
    packs = (low, high)

    def line(yp, total):
        rows = pl.ds(pl.multiple_of(yp * GROUP, GROUP), GROUP)
        present = wide(mask[rows, :])
        for z in range(2):
            for py in range(2):
                for h in range(4):
                    stage[z * 8 + py * 4 + h, 0:28, :] = density[z, 2 * yp + py, :, h * 128 : h * 128 + 128].astype(F32)
        for z in range(2):
            for py in range(2):
                for px in range(2):
                    part = jnp.concatenate(
                        [stage[z * 8 + py * 4 + h, pl.ds(px, GROUP, stride=2), :] for h in range(4)], axis=1
                    )
                    part = part * present
                    total = total + part
                    packs[z][py * 2 + px, rows, 0:PTS] = part.astype(BF16)
        return total

    total = lax.fori_loop(0, LINES, line, jnp.zeros((GROUP, PTS), F32), unroll=4)
    partial[...] = jnp.broadcast_to(jnp.sum(total), partial.shape)
    for z in range(2):
        found = mul(packs[z][:, :, 0:PTS].reshape(4 * ROWS, PTS), anterpolate[...]).astype(BF16)
        found = found.reshape(4, ROWS, K)
        low[:, :, PTS + z * K : PTS + z * K + K] = found
        high[:, :, PTS + z * K : PTS + z * K + K] = found
    parents[...] = merged(low, merge)


def merged(pack, merge):
    children = [pack[c % 4, :, PTS + (c // 4) * K : PTS + (c // 4) * K + K] for c in range(8)]
    return mul(jnp.concatenate(children, axis=1), merge[...]).astype(BF16)


def prologue(density, mask, anterpolate, merge):
    pack = jax.ShapeDtypeStruct((4, ROWS, PTS + 2 * K), BF16)
    return pl.pallas_call(
        prologue_kernel,
        name="prologue",
        out_shape=(
            pack,
            pack,
            jax.ShapeDtypeStruct((ROWS, K), BF16),
            jax.ShapeDtypeStruct((128, 128), F32),
        ),
        in_specs=[VMEM] * 4,
        out_specs=(VMEM,) * 4,
        scratch_shapes=[pltpu.VMEM((16, 32, 128), F32)],
        compiler_params=pltpu.CompilerParams(vmem_limit_bytes=32 << 20),
    )(density, mask, anterpolate, merge)


KEPT = [(3, 0), (3, 1), (3, 2), (3, 3), (1, 3), (2, 3), (1, 1), (1, 2), (2, 1), (2, 2)]
MIRROR = (3, 1, 2, 0)


def taps(before, centre, after):
    ends = before + after
    return [before, 0.5 * (ends + centre), 0.5 * (ends - centre), after]


def outer_weights(tables, outer):
    def chunk(r, _):
        rows = pl.ds(pl.multiple_of(r * 16, 16), 16)
        for h in range(4):
            lanes = slice(h * 128, h * 128 + 128)
            g = [tables[5 + n, rows, lanes].astype(F32) for n in range(9)]
            along_x = [taps(*g[3 * y : 3 * y + 3]) for y in range(3)]
            for c in range(4):
                along_y = taps(along_x[0][c], along_x[1][c], along_x[2][c])
                for b in range(4):
                    outer[b * 4 + c, rows, lanes] = along_y[b].astype(BF16)
        return 0

    lax.fori_loop(0, PTS // 16, chunk, 0, unroll=4)


def inner_weights(tables, outer, inner):
    def block(n, _):
        here = pl.ds(pl.multiple_of((n // 4) * 128, 128), 128)
        there = pl.ds(pl.multiple_of((n % 4) * 128, 128), 128)
        t = [tables[m, here, there].astype(F32) for m in range(5)]
        f = [None] + [tables[m, there, here].T.astype(F32) for m in range(1, 5)]
        above = taps(t[2], t[3], t[4])
        below = taps(f[4], f[3], f[2])
        level = taps(f[1], t[0], t[1])
        for k, (b, c) in enumerate(KEPT):
            if b == 3:
                flat = above[c]
            elif b == 1:
                flat = 0.5 * (below[c] + above[c] + level[c])
            else:
                flat = 0.5 * (below[c] + above[c] - level[c])
            ends = outer[b * 4 + c, here, there].astype(F32)
            ends = ends + outer[MIRROR[b] * 4 + MIRROR[c], there, here].T.astype(F32)
            inner[k, here, there] = (0.5 * (ends + flat)).astype(BF16)
            inner[10 + k, here, there] = (0.5 * (ends - flat)).astype(BF16)
        return 0

    lax.fori_loop(0, 16, block, 0, unroll=4)


def spread_line(load, store):
    along_y = []
    for px in range(2):
        d0 = load(1, px, -1)
        d1 = load(0, px, 0)
        d2 = load(1, px, 0)
        d3 = load(0, px, 1)
        along_y.append((d0 - d2, d1 + d2, d2 - d1, d1 - d3))
    for b in range(4):
        even = along_y[0][b]
        odd = along_y[1][b]
        store(b * 4 + 0, pltpu.roll(odd, 1, axis=0) - odd)
        store(b * 4 + 1, even + odd)
        store(b * 4 + 2, odd - even)
        store(b * 4 + 3, even - pltpu.roll(even, GROUP - 1, axis=0))


def spread(first, second, combine, spread_ref, base):
    def line(yp, _):
        rows = pl.ds(pl.multiple_of(yp * GROUP, GROUP), GROUP)
        for h in range(4):
            lanes = slice(h * 128, h * 128 + 128)

            def load(py, px, shift):
                near_line = jnp.clip(yp + shift, 0, LINES - 1)
                at = pl.ds(pl.multiple_of(near_line * GROUP, GROUP), GROUP)
                found = combine(
                    first[py * 2 + px, at, lanes].astype(F32), second[py * 2 + px, at, lanes].astype(F32)
                )
                if shift == 0:
                    return found
                inside = (yp + shift >= 0) & (yp + shift < LINES)
                return jnp.where(inside, found, 0.0)

            def store(n, value):
                spread_ref[base + n, rows, lanes] = value.astype(BF16)

            spread_line(load, store)
        return 0

    lax.fori_loop(0, LINES, line, 0, unroll=4)


def gathered_products(product, held, made):
    for b in range(4):
        for c in range(4):
            made[4 * b + c] = product(b, c)
        p = [made[4 * b + c] for c in range(4)]
        sides = (p[0] + p[1] + p[2], p[1] - p[2] - p[3])
        for px in range(2):
            value = sides[px]
            if b == 0:
                held[0, px] = value
            elif b == 1:
                held[0, px] += value
                held[1, px] = value
            elif b == 2:
                held[0, px] += value
                held[1, px] -= value
            else:
                held[1, px] -= value


def near_inner_kernel(low, high, tables_in, near, outer_out, parts, inner, held, made, tables, outer, sems):
    ends = pltpu.make_async_copy(tables_in.at[5:14], tables.at[5:14], sems.at[0])
    flats = pltpu.make_async_copy(tables_in.at[0:5], tables.at[0:5], sems.at[1])
    ends.start()
    flats.start()
    spread(low, high, lambda d1, d2: d1 + d2, parts, 0)
    spread(low, high, lambda d1, d2: d2 - d1, parts, 16)
    ends.wait()
    outer_weights(tables, outer)
    leaving = pltpu.make_async_copy(outer, outer_out, sems.at[2])
    leaving.start()
    flats.wait()
    inner_weights(tables, outer, inner)

    def product(a):
        def one(b, c):
            left = parts[a * 16 + b * 4 + c]
            if (b, c) in KEPT:
                return mul(left, inner[a * 10 + KEPT.index((b, c))])
            return mul_t(left, inner[a * 10 + KEPT.index((MIRROR[b], MIRROR[c]))])

        return one

    for a in range(2):
        gathered_products(product(a), held.at[a], made)
    near[0] = held[0] + held[1]
    near[1] = held[0] - held[1]
    leaving.wait()


def near_inner(low, high, tables):
    return pl.pallas_call(
        near_inner_kernel,
        name="near_inner",
        out_shape=(
            jax.ShapeDtypeStruct((2, 2, 2, ROWS, PTS), F32),
            jax.ShapeDtypeStruct((16, PTS, PTS), BF16),
        ),
        in_specs=[VMEM, VMEM, ANY],
        out_specs=(VMEM, ANY),
        scratch_shapes=[
            pltpu.VMEM((32, ROWS, PTS), BF16),
            pltpu.VMEM((20, PTS, PTS), BF16),
            pltpu.VMEM((2, 2, 2, ROWS, PTS), F32),
            pltpu.VMEM((16, ROWS, PTS), F32),
            pltpu.VMEM((14, PTS, PTS), BF16),
            pltpu.VMEM((16, PTS, PTS), BF16),
            pltpu.SemaphoreType.DMA((3,)),
        ],
        cost_estimate=pl.CostEstimate(flops=10_000_000_000, bytes_accessed=20_000_000, transcendentals=0),
        compiler_params=pltpu.CompilerParams(vmem_limit_bytes=60 << 20),
    )(low, high, tables)


def flags(place, count):
    third = place + 3 - 6 * (place % 2)
    found = (place >= 1, place < count - 1, place >= 2, place < count - 2, (third >= 0) & (third < count))
    return [jnp.where(f, 1.0, 0.0) for f in found]


def near_outer_kernel(count, place, low, high, below, above, outer_in, near_in, near, parts, held, made, outer, sems):
    kept = flags(place[0], count)
    weights = [
        pltpu.make_async_copy(outer_in.at[4 * m : 4 * m + 4], outer.at[4 * m : 4 * m + 4], sems.at[m])
        for m in range(4)
    ]
    inner_part = pltpu.make_async_copy(near_in, near, sems.at[4])
    for b in range(4):
        weights[MIRROR[b]].start()
    inner_part.start()
    spread(below, high, lambda d0, d2: d0 * kept[0] - d2, parts, 0)
    spread(low, above, lambda d1, d3: d1 - d3 * kept[1], parts, 16)
    def mirrored(b, c):
        if c == 0:
            weights[MIRROR[b]].wait()
        return mul_t(parts[b * 4 + c], outer[MIRROR[b] * 4 + MIRROR[c]])

    gathered_products(mirrored, held, made)
    inner_part.wait()
    near[0] += held[...]
    gathered_products(lambda b, c: mul(parts[16 + b * 4 + c], outer[b * 4 + c]), held, made)
    near[1] -= held[...]


def near_outer(count, place, low, high, below, above, outer, near):
    return pl.pallas_call(
        functools.partial(near_outer_kernel, count),
        name="near_outer",
        out_shape=jax.ShapeDtypeStruct((2, 2, 2, ROWS, PTS), F32),
        in_specs=[SMEM] + [VMEM] * 4 + [ANY] * 2,
        out_specs=VMEM,
        scratch_shapes=[
            pltpu.VMEM((32, ROWS, PTS), BF16),
            pltpu.VMEM((2, 2, ROWS, PTS), F32),
            pltpu.VMEM((16, ROWS, PTS), F32),
            pltpu.VMEM((16, PTS, PTS), BF16),
            pltpu.SemaphoreType.DMA((5,)),
        ],
        cost_estimate=pl.CostEstimate(flops=7_000_000_000, bytes_accessed=20_000_000, transcendentals=0),
        compiler_params=pltpu.CompilerParams(vmem_limit_bytes=60 << 20),
    )(place, low, high, below, above, outer, near)


def positive_offsets(radius, minimum):
    reach = range(-radius, radius + 1)
    return [
        (z, y, x)
        for z in reach
        for y in reach
        for x in reach
        if max(abs(z), abs(y), abs(x)) >= minimum and (z, y, x) > (0, 0, 0)
    ]


RANK = {offset: row for row, offset in enumerate(positive_offsets(3, 2))}


def transfer_terms(tables, dz, reach, py, source):
    plain, flipped = ([], []), ([], [])
    blank = jnp.zeros((K, K), BF16)
    for jy in reach:
        dy = jy - py
        for jx in range(-2, 4):
            pair = []
            for px in range(2):
                offset = (dz, dy, jx - px)
                other = tuple(-d for d in offset)
                pair.append((RANK.get(offset), RANK.get(other)))
            left = None
            for way, kept in ((0, plain), (1, flipped)):
                if pair[0][way] is None and pair[1][way] is None:
                    continue
                left = source(jy, jx) if left is None else left
                kept[0].append(left)
                kept[1].append(
                    jnp.concatenate(
                        [blank if q[way] is None else tables[q[way]] for q in pair], axis=1 - way
                    )
                )
    terms = []
    if plain[0]:
        terms.append(mul(jnp.concatenate(plain[0], axis=1), jnp.concatenate(plain[1], axis=0)))
    if flipped[0]:
        terms.append(mul_t(jnp.concatenate(flipped[0], axis=1), jnp.concatenate(flipped[1], axis=1)))
    return terms


def neighbours(even, odd, count):
    return jnp.concatenate(
        [
            pltpu.roll(even, 1, axis=0),
            pltpu.roll(odd, 1, axis=0),
            even,
            odd,
            pltpu.roll(even, count - 1, axis=0),
            pltpu.roll(odd, count - 1, axis=0),
        ],
        axis=1,
    ).astype(BF16)


def coarse_lines(box, stage, slot, lines):
    stage[...] = box
    sides = []
    for py in range(2):
        halves = []
        for px in range(2):
            halves.append(
                jnp.concatenate(
                    [stage[pl.ds(32 * g + 16 * py + px, 8, stride=2), :] for g in range(6)], axis=0
                )
            )
        sides.append(halves)
    blank = jnp.zeros((8, K), F32)
    for jy in range(-2, 4):
        even, odd = sides[jy % 2]
        if jy // 2 < 0:
            even, odd = [jnp.concatenate([blank, h[: COARSE - 8]], axis=0) for h in (even, odd)]
        elif jy // 2 > 0:
            even, odd = [jnp.concatenate([h[8:], blank], axis=0) for h in (even, odd)]
        lines[slot, jy + 2] = neighbours(even, odd, COARSE)


def transfer_kernel(
    count, place, low, below, above, own, back2, ahead2, far3, mask, charge, merge, anterpolate, tables_in, near_in,
    potential, leaves, lines, stage, weave, flat, coarse, tables, near, fine, sems,
):
    kept = flags(place[0], count)
    operators = pltpu.make_async_copy(tables_in, tables, sems.at[0])
    near_part = pltpu.make_async_copy(near_in, near, sems.at[1])
    operators.start()
    near_part.start()
    packs = (below, below, low, low, above, above)
    leaves[...] = jnp.zeros_like(leaves)
    for n in range(6):
        first = PTS + (n % 2) * K
        for py in range(2):
            even = packs[n][py * 2, :, first : first + K].astype(F32)
            odd = packs[n][py * 2 + 1, :, first : first + K].astype(F32)
            if n < 2 or n > 3:
                even, odd = even * kept[n // 4], odd * kept[n // 4]
            leaves[n, py, GROUP : GROUP + ROWS, :] = neighbours(even, odd, ROWS)
    side = place[0] % 2
    boxes = (back2[...], merged(below, merge), own[...], merged(above, merge), ahead2[...])
    for n, (box, flag) in enumerate(zip(boxes, (2, 0, None, 1, 3))):
        box = box.astype(F32)
        coarse_lines(box if flag is None else box * kept[flag], stage, n + side, lines)
    coarse_lines(far3[...].astype(F32) * kept[4], stage, 5 - 5 * side, lines)

    operators.wait()
    coarse[...] = jnp.zeros_like(coarse)
    fine[...] = jnp.zeros_like(fine)
    for py in range(2):
        for dz in range(-3, 4):
            layers = [pz for pz in range(2) if -2 <= dz + pz <= 3]
            slot = jnp.clip(dz + side + 2, 0, 5)

            def source(jy, jx):
                lines_here = pl.ds(GROUP * (1 + jy // 2), ROWS)
                lanes = slice((jx + 2) * K, (jx + 3) * K)
                here = [leaves[dz + pz + 2, jy % 2, lines_here, lanes] for pz in layers]
                return jnp.concatenate(here + [lines[slot, jy + 2, :, lanes]], axis=0)

            for term in transfer_terms(tables, dz, range(-2, 4), py, source):
                for n, pz in enumerate(layers):
                    fine[pz * 2 + py] += term[n * ROWS : n * ROWS + ROWS]
                wider = term[len(layers) * ROWS :]
                if abs(dz) == 3:
                    wider = jnp.where(side == (dz < 0), wider, 0.0)
                coarse[py] += 0.5 * wider

    for py in range(2):
        for px in range(2):
            for g in range(6):
                stage[pl.ds(32 * g + 16 * py + px, 8, stride=2), :] = coarse[
                    py, g * 8 : g * 8 + 8, px * K : px * K + K
                ]
    parent_local = stage[...].astype(BF16)

    total_charge = jnp.sum(charge[...], axis=0, keepdims=True)
    leaf_count = 2.0 * 24 * 28 * 128
    factor = wide(mask[...] * (leaf_count * PTS / total_charge))

    near_part.wait()
    for pz in range(2):
        for py in range(2):
            first = (4 * pz + 2 * py) * K
            total = fine[pz * 2 + py] + mul_t(parent_local, merge[first : first + 2 * K, :])
            local = total.astype(BF16)
            for px in range(2):
                far = mul_t(local[:, px * K : px * K + K], anterpolate[...])
                found = (near[pz, py, px] + far) * factor
                for h in range(4):
                    flat[px, h] = found[:, h * 128 : h * 128 + 128]
                for xp in range(14):
                    for h in range(4):
                        weave[h, 2 * xp + px, pl.ds(py, LINES, stride=2), :] = flat[px, h, pl.ds(xp, LINES, stride=GROUP), :]
        for x in range(28):
            for h in range(4):
                potential[pz, x, :, h * 128 : h * 128 + 128] = weave[h, x].astype(BF16)


def transfer(count, place, low, below, above, own, back2, ahead2, far3, mask, charge, merge, anterpolate, tables, near):
    return pl.pallas_call(
        functools.partial(transfer_kernel, count),
        name="transfer",
        out_shape=jax.ShapeDtypeStruct((2, 28, 2 * LINES, PTS), BF16),
        in_specs=[SMEM] + [VMEM] * 11 + [ANY] * 2,
        out_specs=VMEM,
        scratch_shapes=[
            pltpu.VMEM((6, 2, ROWS + 2 * GROUP, 6 * K), BF16),
            pltpu.VMEM((6, 6, COARSE, 6 * K), BF16),
            pltpu.VMEM((ROWS, K), F32),
            pltpu.VMEM((4, 28, 2 * LINES, 128), F32),
            pltpu.VMEM((2, 4, ROWS, 128), F32),
            pltpu.VMEM((2, COARSE, 2 * K), F32),
            pltpu.VMEM((len(RANK), K, K), BF16),
            pltpu.VMEM((2, 2, 2, ROWS, PTS), F32),
            pltpu.VMEM((4, ROWS, 2 * K), F32),
            pltpu.SemaphoreType.DMA((2,)),
        ],
        cost_estimate=pl.CostEstimate(flops=12_000_000_000, bytes_accessed=20_000_000, transcendentals=0),
        compiler_params=pltpu.CompilerParams(vmem_limit_bytes=60 << 20),
    )(place, low, below, above, own, back2, ahead2, far3, mask, charge, merge, anterpolate, tables, near)


def around(count, step):
    return [(i, (i + step) % count) for i in range(count)]


def body(density, occupied, anterpolate, merge_tables, transfer_tables, near_tables):
    count = lax.axis_size("leaf")
    present = jnp.pad(occupied[0].astype(F32), ((0, 0), (0, GROUP - occupied.shape[2])))
    mask = jnp.broadcast_to(present.reshape(ROWS, 1), (ROWS, 128))
    merge = merge_tables.reshape(8 * K, K)
    low, high, own, partial = prologue(density, mask, anterpolate, merge)
    place = lax.axis_index("leaf").reshape(1)
    below = lax.ppermute(high, "leaf", around(count, 1))
    above = lax.ppermute(low, "leaf", around(count, -1))
    charge = lax.all_to_all(partial, "leaf", 0, 0, tiled=True)
    near, outer = near_inner(low, high, near_tables)
    own, near = lax.optimization_barrier((own, near))
    back2 = lax.ppermute(own, "leaf", around(count, 2))
    ahead2 = lax.ppermute(own, "leaf", around(count, -2))
    crossed = [(i, (i + 3) % count) for i in range(0, count, 2)]
    far3 = lax.ppermute(own, "leaf", crossed + [(j, i) for i, j in crossed])
    near = near_outer(count, place, low, high, below, above, outer, near)
    potential = transfer(
        count, place, low, below, above, own, back2, ahead2, far3, mask, charge, merge, anterpolate,
        transfer_tables, near,
    )
    return jnp.swapaxes(potential, 1, 2)


def solution(mesh):
    return jax.shard_map(
        body,
        mesh=mesh,
        in_specs=(P("leaf", None, None, None), P("leaf", None, None), P(), P(), P(), P()),
        out_specs=P("leaf", None, None, None),
        check_vma=False,
    )
```
